256 devices in a mesh: dp: 4 (over x), ctx: 64 (over z, y, core).
Axes of the slice: x: 4, y: 4, z: 8, core: 2. Of those that a mesh axis runs over, the one named last changes fastest.
Arguments:
- raw_qkv: bfloat16 [4, 3, 4096, 10240], P('dp', None, None, 'ctx'), may hold values from -6 to 6
- block_lengths: int32 [4, 64, 2], P('dp', 'ctx'), may hold values from 1 to 159, as said below
- short_filter: float32 [3, 256, 7], replicated, may hold values from -2 to 2
- medium_filter: float32 [256, 64], replicated, may hold values from -0.75 to 0.75
- doc_span: int32 [4, 2, 8192], P('dp', None, 'ctx'), may hold values from 0 to 285, as said below
- cotangent: bfloat16 [4, 4096, 8192], P('dp', None, 'ctx'), may hold values from -6 to 6
Outputs:
- grad_qkv: bfloat16 [4, 3, 4096, 8192], P('dp', None, None, 'ctx')
- grad_short: float32 [3, 256, 7], replicated
- grad_medium: float32 [256, 64], replicated
The draws below stay inside these ranges and needn't reach their ends.
Inputs may be any that keep to these rules, and one draw needn't show every extreme that they name: Entry k of block_lengths[n, i] is the length of the k-th document piece among the live rows of block i, which are its first live[n, i] rows. The first piece of every block but block 0 continues the document that ends the block before. start[n, i] differs from i * 128 by at most 16; in every sequence some block starts 16 rows late and another 16 rows early. All blocks of a sequence together hold 8192 live rows. `doc_span`: row 0 counts the tokens of the same document before a packed token, row 1 those after it, for the documents that block_lengths describes.
All inputs are finite; a program needn't handle non-finite values.
Results may differ from the reference program's by a relative error of at most 0.008.
Values may be sent and summed in bfloat16 or wider, within the bound.
A program may use at most 192 MiB of HBM per device.

```python
import jax
import jax.numpy as jnp
from jax import lax

WIDTH = 4096
GROUP = 16
SHORT = 7
MED = 64
ROWS = 128
PIECES = 2
GROUPS = 256
DRIFT = 16
CAP = 160
TOKENS = 8192
SAMPLES = 524288
N_DP = 4
N_CTX = 64


def layout_one(key):
    key_drift, key_place, key_cut = jax.random.split(key, 3)
    inner = jax.random.randint(key_drift, (N_CTX - 1,), -DRIFT, DRIFT + 1).astype(jnp.int32)
    anchor = jax.random.randint(key_place, (), 0, N_CTX - 3).astype(jnp.int32)
    slots = jnp.arange(N_CTX - 1, dtype=jnp.int32)
    raised = (slots == anchor + 1) | (slots == anchor + 2)
    inner = jnp.where(slots == anchor, -DRIFT, jnp.where(raised, DRIFT, inner)).astype(jnp.int32)
    border = jnp.zeros((1,), jnp.int32)
    excess = jnp.concatenate([border, inner, border])
    counts = (ROWS + excess[1:] - excess[:-1]).astype(jnp.int32)
    places = jnp.arange(CAP, dtype=jnp.int32)[None, :]
    blocks = jnp.arange(N_CTX, dtype=jnp.int32)[:, None]
    scores = jax.random.randint(key_cut, (N_CTX, CAP), 0, 65536).astype(jnp.int32) * CAP + places
    scores = jnp.where((places >= 1) & (places < counts[:, None]), scores, -1)
    early_cuts = (blocks == anchor + 1) & (places >= 1) & (places < PIECES)
    late_cuts = (blocks == anchor + 2) & (places >= counts[:, None] - PIECES + 1) & (places < counts[:, None])
    scores = jnp.where(early_cuts | late_cuts, 65536 * CAP + places, scores).astype(jnp.int32)
    cuts = jnp.sort(lax.top_k(scores, PIECES - 1)[0] % CAP, axis=1).astype(jnp.int32)
    bounds = jnp.concatenate([jnp.zeros((N_CTX, 1), jnp.int32), cuts, counts[:, None]], axis=1)
    lengths = bounds[:, 1:] - bounds[:, :-1]
    starts = jnp.cumsum(counts) - counts
    piece_starts = starts[:, None] + bounds[:, :-1]
    opening = (jnp.arange(PIECES)[None, :] > 0) | (jnp.arange(N_CTX)[:, None] == 0)
    marks = jnp.where(opening, piece_starts, -1).reshape(-1)[None, :]
    tokens = jnp.arange(TOKENS, dtype=jnp.int32)[:, None]
    last_open = jnp.max(jnp.where((marks >= 0) & (marks <= tokens), marks, -1), axis=1)
    next_open = jnp.min(jnp.where(marks > tokens, marks, TOKENS), axis=1)
    before = tokens[:, 0] - last_open
    after = next_open - 1 - tokens[:, 0]
    return (lengths.astype(jnp.int32), jnp.stack([before, after]).astype(jnp.int32))


def layout(key):
    return jax.vmap(layout_one)(jax.random.split(key, N_DP))


def draw_block_lengths(key, part):
    lengths, spans = layout(key)
    return lengths


def draw_doc_span(key, part):
    lengths, spans = layout(key)
    return spans


def block_scale(key, extent, cuts, least, high):
    level = 1.0
    for axis_at, parts in cuts:
        draws = jax.random.uniform(jax.random.fold_in(jax.random.fold_in(key, 6), axis_at), (parts,), jnp.float32, least / len(cuts), high / len(cuts))
        level = level * jnp.repeat(jnp.exp(draws), extent[axis_at] // parts).reshape((-1,) + (1,) * (len(extent) - 1 - axis_at))
    return level


def noise(own_key, shape, width, most, cuts=(), kind=jnp.bfloat16):
    level = block_scale(own_key, shape, cuts, -0.22, 0.18) if cuts else 1.0
    result = jax.random.normal(own_key, shape, jnp.float32) * width * level
    return jnp.minimum(jnp.maximum(result, -most), most).astype(kind)


def setup_inputs(seed: int = 0) -> dict:
    key_of = jax.random.split(jax.random.key(seed), 7)
    raw_qkv = noise(key_of[0], (N_DP, 3, WIDTH, CAP * N_CTX), 1.0, 6.0, ((0, 4), (3, 64)))
    block_lengths = draw_block_lengths(jax.random.fold_in(key_of[6], 71), 0)
    short_filter = noise(key_of[2], (3, GROUPS, SHORT), SHORT ** -0.5, 2.0, (), jnp.float32)
    medium_filter = noise(key_of[3], (GROUPS, MED), MED ** -0.5, 0.75, (), jnp.float32)
    doc_span = draw_doc_span(jax.random.fold_in(key_of[6], 71), 0)
    cotangent = noise(key_of[5], (N_DP, WIDTH, TOKENS), 1.0, 6.0, ((0, 4), (2, 64)))
    return {"raw_qkv": raw_qkv, "block_lengths": block_lengths, "short_filter": short_filter, "medium_filter": medium_filter, "doc_span": doc_span, "cotangent": cotangent}


HIGH = lax.Precision.HIGHEST

def as_rounded(weights):
    narrowed = lax.optimization_barrier(weights.astype(jnp.bfloat16))
    return narrowed.astype(jnp.float32)

def pack_sequence(raw_rows, lengths):
    counts = lax.optimization_barrier(jnp.sum(lengths, axis=1)).astype(jnp.int32)
    starts = (jnp.cumsum(counts) - counts).astype(jnp.int32)
    position = jnp.arange(TOKENS, dtype=jnp.int32)
    owner = (lax.optimization_barrier(jnp.sum((starts[None, :] <= position[:, None]).astype(jnp.int32), axis=1)) - 1).astype(jnp.int32)
    within = (position - jnp.take(starts, owner)).astype(jnp.int32)
    column = (owner * CAP + within).astype(jnp.int32)
    return jnp.take(raw_rows, column, axis=2)

def short_forward(packed, short_wide, before):
    padded = jnp.pad(packed.astype(jnp.float32), ((0, 0), (0, 0), (SHORT - 1, 0)))
    summed = jnp.zeros(packed.shape, jnp.float32)
    for tap_lag in range(SHORT):
        window = padded[:, :, SHORT - 1 - tap_lag:SHORT - 1 - tap_lag + TOKENS]
        summed = summed + jnp.where(tap_lag <= before, short_wide[:, :, tap_lag:tap_lag + 1] * window, 0.0)
    return summed

def medium_block(window, medium_taps, before):
    out_index = jnp.arange(ROWS, dtype=jnp.int32)[:, None]
    in_index = jnp.arange(ROWS + MED - 1, dtype=jnp.int32)[None, :]
    tap_lag = (out_index + MED - 1 - in_index).astype(jnp.int32)
    allowed = (tap_lag >= 0) & (tap_lag < MED) & (tap_lag <= before[:, None])
    picked = jnp.take(medium_taps, jnp.clip(tap_lag, 0, MED - 1).astype(jnp.int32), axis=1)
    matrix = jnp.where(allowed[None], picked, 0.0)
    grouped = window.reshape(GROUPS, GROUP, ROWS + MED - 1)
    return jnp.einsum('gcu,gtu->gct', grouped, matrix, precision=HIGH).reshape(WIDTH, ROWS)

def medium_forward(signal, medium_taps, before):
    padded = jnp.pad(signal, ((0, 0), (MED - 1, 0)))

    def block_out(number):
        window = lax.dynamic_slice_in_dim(padded, number * ROWS, ROWS + MED - 1, 1)
        local_before = lax.dynamic_slice_in_dim(before, number * ROWS, ROWS, 0)
        return medium_block(window, medium_taps, local_before)
    blocks = lax.map(jax.checkpoint(block_out), jnp.arange(TOKENS // ROWS, dtype=jnp.int32))
    return jnp.transpose(blocks, (1, 0, 2)).reshape(WIDTH, TOKENS)

def sequence(raw_rows, lengths, span, upstream, short_taps, medium_taps):
    packed = pack_sequence(raw_rows, lengths)
    before = span[0]
    short_wide = jnp.repeat(short_taps, GROUP, axis=1)
    filtered = short_forward(packed, short_wide, before)
    mixed = (filtered[1] * filtered[2]).astype(jnp.bfloat16)

    def medium_of(signal, weights):
        return medium_forward(signal, weights, before)
    response, pullback = jax.vjp(medium_of, mixed.astype(jnp.float32), medium_taps)
    upstream32 = upstream.astype(jnp.float32)
    weighted = (upstream32 * filtered[0]).astype(jnp.bfloat16)
    grad_query = upstream32 * response
    spread, medium_grad = pullback(weighted.astype(jnp.float32))
    grad_filtered = jnp.stack([grad_query, spread * filtered[2], spread * filtered[1]]).astype(jnp.bfloat16)
    grad_wide = grad_filtered.astype(jnp.float32)
    later = jnp.pad(grad_wide, ((0, 0), (0, 0), (0, SHORT - 1)))
    later_before = jnp.pad(before, (0, SHORT - 1), constant_values=-1)
    earlier = jnp.pad(packed.astype(jnp.float32), ((0, 0), (0, 0), (SHORT - 1, 0)))
    grad_inputs = jnp.zeros(grad_wide.shape, jnp.float32)
    short_terms = []
    for tap_lag in range(SHORT):
        ahead = later[:, :, tap_lag:tap_lag + TOKENS]
        allowed = tap_lag <= later_before[tap_lag:tap_lag + TOKENS]
        grad_inputs = grad_inputs + jnp.where(allowed, short_wide[:, :, tap_lag:tap_lag + 1] * ahead, 0.0)
        behind = earlier[:, :, SHORT - 1 - tap_lag:SHORT - 1 - tap_lag + TOKENS]
        per_channel = lax.optimization_barrier(jnp.sum(jnp.where(tap_lag <= before, grad_wide * behind, 0.0), axis=2))
        short_terms.append(lax.optimization_barrier(jnp.sum(per_channel.reshape(3, GROUPS, GROUP), axis=2)))
    return (grad_inputs.astype(jnp.bfloat16), jnp.stack(short_terms, axis=2), medium_grad)

def reference(raw_qkv, block_lengths, short_filter, medium_filter, doc_span, cotangent):
    short_taps = as_rounded(short_filter)
    medium_taps = as_rounded(medium_filter)

    def one_sequence(operands):
        raw_rows, lengths, span, upstream = operands
        return sequence(raw_rows, lengths, span, upstream, short_taps, medium_taps)
    grads, short_parts, medium_parts = lax.map(one_sequence, (raw_qkv, block_lengths, doc_span, cotangent))
    scale = jnp.sqrt(jnp.float32(SAMPLES))
    return (grads, lax.optimization_barrier(jnp.sum(short_parts, axis=0)) / scale, lax.optimization_barrier(jnp.sum(medium_parts, axis=0)) / scale)
```

```python
import functools
import math

import jax
import jax.numpy as jnp
from jax import lax
from jax.experimental import pallas as pl
from jax.experimental.pallas import tpu as pltpu
from jax.sharding import PartitionSpec as P

F32 = jnp.float32
BF16 = jnp.bfloat16
MESH = pl.DeviceIdType.MESH
LANES = 128
REACH = 22
TAIL_ROWS = 80
HEAD_ROWS = 16
LEAD = 8
HALF = 64


def iota(shape, dim):
    return lax.broadcasted_iota(jnp.int32, shape, dim)


def ones_where(condition, dtype=BF16):
    return jnp.where(condition, 1.0, 0.0).astype(dtype)


def dot(left, right):
    return jnp.dot(left, right, preferred_element_type=F32)


def dot_rows(left, right):
    return lax.dot_general(left, right, (((1,), (1,)), ((), ())), preferred_element_type=F32)


def column_of(row):
    return jnp.transpose(jnp.broadcast_to(row, (LANES, LANES)))


def tail_kernel(lengths_ref, raw_ref, tail_ref):
    live = lengths_ref[0, 0] + lengths_ref[0, 1]
    cap = raw_ref.shape[1]
    place = iota((TAIL_ROWS, cap), 0)
    column = iota((TAIL_ROWS, cap), 1)
    total = None
    for part in range(3):
        step = place - REACH * part
        pick = ones_where((step >= 0) & (step < REACH) & (column == live - REACH + step))
        term = dot(pick, raw_ref[part])
        total = term if total is None else total + term
    tail_ref[...] = total.astype(BF16)


def build_tail(lengths, raw, block=512):
    width = raw.shape[2]
    return pl.pallas_call(
        tail_kernel,
        grid=(width // block,),
        in_specs=[
            pl.BlockSpec(memory_space=pltpu.SMEM),
            pl.BlockSpec((3, raw.shape[1], block), lambda i: (0, 0, i)),
        ],
        out_specs=pl.BlockSpec((TAIL_ROWS, block), lambda i: (0, i)),
        out_shape=jax.ShapeDtypeStruct((TAIL_ROWS, width), BF16),
    )(lengths, raw)


def start_kernel(inner, lengths_ref, start_ref, mine, near, far, send, near_sem, far_sem):
    me = lax.axis_index("ctx")
    outer = lax.axis_size("ctx") // inner
    col, row = lax.rem(me, inner), lax.div(me, inner)
    barrier = pltpu.get_barrier_semaphore()
    for hop in range(1, inner):
        peer = row * inner + lax.rem(col + hop, inner)
        pl.semaphore_signal(barrier, inc=1, device_id={"ctx": peer}, device_id_type=MESH)
    for hop in range(1, outer):
        peer = lax.rem(row + hop, outer) * inner + col
        pl.semaphore_signal(barrier, inc=1, device_id={"ctx": peer}, device_id_type=MESH)
    pl.semaphore_wait(barrier, inner + outer - 2)
    lengths = lengths_ref[...]
    live = jnp.broadcast_to(lengths[0:1, 0:1] + lengths[0:1, 1:2], (8, LANES))
    mine[0] = live
    copies = []
    for hop in range(1, inner):
        peer = row * inner + lax.rem(col + hop, inner)
        copy = pltpu.make_async_remote_copy(
            mine.at[0],
            near.at[inner - hop],
            send.at[hop],
            near_sem.at[inner - hop],
            device_id={"ctx": peer},
            device_id_type=MESH,
        )
        copy.start()
        copies.append(copy)
    for copy in copies:
        copy.wait()
    before = jnp.zeros((8, LANES), jnp.int32)
    whole = live
    for hop in range(1, inner):
        value = near[hop]
        whole = whole + value
        before = before + value * jnp.where(col + hop >= inner, 1, 0)
    mine[1] = whole
    copies = []
    for hop in range(1, outer):
        peer = lax.rem(row + hop, outer) * inner + col
        copy = pltpu.make_async_remote_copy(
            mine.at[1],
            far.at[outer - hop],
            send.at[inner + hop],
            far_sem.at[outer - hop],
            device_id={"ctx": peer},
            device_id_type=MESH,
        )
        copy.start()
        copies.append(copy)
    for copy in copies:
        copy.wait()
    for hop in range(1, outer):
        before = before + far[hop] * jnp.where(row + hop >= outer, 1, 0)
    start_ref[...] = before


def block_start(lengths, inner=8):
    outer = lax.axis_size("ctx") // inner
    return pl.pallas_call(
        functools.partial(start_kernel, inner),
        in_specs=[pl.BlockSpec(memory_space=pltpu.VMEM)],
        out_specs=pl.BlockSpec(memory_space=pltpu.VMEM),
        out_shape=jax.ShapeDtypeStruct((8, LANES), jnp.int32),
        scratch_shapes=[
            pltpu.VMEM((2, 8, LANES), jnp.int32),
            pltpu.VMEM((inner, 8, LANES), jnp.int32),
            pltpu.VMEM((outer, 8, LANES), jnp.int32),
            pltpu.SemaphoreType.DMA((inner + outer,)),
            pltpu.SemaphoreType.DMA((inner,)),
            pltpu.SemaphoreType.DMA((outer,)),
        ],
        compiler_params=pltpu.CompilerParams(collective_id=0, has_side_effects=True),
    )(lengths)


def widened_taps(short_ref, block, lanes):
    groups = short_ref.shape[2]
    spread = ones_where(iota((groups, lanes), 0) == (block * lanes + iota((groups, lanes), 1)) // 16)
    return [dot(short_ref[part].astype(BF16), spread) for part in range(3)]


def forward_kernel(
    drift_ref,
    lengths_ref,
    raw_ref,
    tail_ref,
    head_ref,
    short_ref,
    span_ref,
    cot_ref,
    packed_ref,
    cot_out_ref,
    filtered_ref,
    mixed_ref,
    weighted_ref,
    own_pick,
    edge_pick,
    masks,
    rows,
):
    cap = raw_ref.shape[1]
    count = cot_ref.shape[1]
    block = pl.program_id(0)

    @pl.when(block == 0)
    def _():
        drift = drift_ref[0, 0]
        live = lengths_ref[0, 0] + lengths_ref[0, 1]
        token = iota((LEAD + count, cap), 0) - LEAD
        column = iota((LEAD + count, cap), 1)
        own_pick[...] = ones_where((column == token - drift) & (column < live))
        token = iota((LEAD + count, LANES), 0) - LEAD
        column = iota((LEAD + count, LANES), 1)
        for part in range(3):
            late = token - drift + REACH
            from_tail = (late >= 0) & (late < REACH) & (column == REACH * part + late)
            over = token - drift - live
            from_head = (over >= 0) & (column == TAIL_ROWS + HEAD_ROWS * part + over)
            edge_pick[part] = ones_where(from_tail | from_head)
        before = column_of(span_ref[0:1])
        for lag in range(1, 7):
            masks[lag - 1] = ones_where(before >= lag, F32)

    taps = widened_taps(short_ref, block, LANES)
    edges = jnp.concatenate([tail_ref[...]] + [head_ref[part] for part in range(3)], axis=0)
    filtered = []
    for part in range(3):
        packed = dot(own_pick[...], raw_ref[part]) + dot(edge_pick[part], edges)
        rows[part] = packed
        packed_ref[part] = packed[LEAD:].astype(BF16)
        total = taps[part][0:1] * packed[LEAD:]
        for lag in range(1, 7):
            window = rows[part, LEAD - lag : LEAD - lag + count]
            total = total + taps[part][lag : lag + 1] * (masks[lag - 1] * window)
        filtered.append(total)
    filtered_ref[0] = filtered[1]
    filtered_ref[1] = filtered[2]
    mixed_ref[...] = (filtered[1] * filtered[2]).astype(BF16)
    cot = jnp.transpose(cot_ref[...].astype(F32))
    cot_out_ref[...] = cot.astype(BF16)
    weighted_ref[...] = (cot * filtered[0]).astype(BF16)


def forward(drift, lengths, raw, tail, head, short, span, cot):
    cap, width = raw.shape[1:]
    count = cot.shape[1]
    smem = pl.BlockSpec(memory_space=pltpu.SMEM)
    by_lane = lambda *lead: pl.BlockSpec(lead + (LANES,), lambda i: (0,) * len(lead) + (i,))
    whole = lambda a: pl.BlockSpec(a.shape, lambda i: (0,) * a.ndim)
    return pl.pallas_call(
        forward_kernel,
        grid=(width // LANES,),
        in_specs=[
            smem,
            smem,
            by_lane(3, cap),
            by_lane(TAIL_ROWS),
            by_lane(3, HEAD_ROWS),
            whole(short),
            whole(span),
            pl.BlockSpec((LANES, count), lambda i: (i, 0)),
        ],
        out_specs=[
            by_lane(3, count),
            by_lane(count),
            by_lane(2, count),
            by_lane(count),
            by_lane(count),
        ],
        out_shape=[
            jax.ShapeDtypeStruct((3, count, width), BF16),
            jax.ShapeDtypeStruct((count, width), BF16),
            jax.ShapeDtypeStruct((2, count, width), F32),
            jax.ShapeDtypeStruct((count, width), BF16),
            jax.ShapeDtypeStruct((count, width), BF16),
        ],
        scratch_shapes=[
            pltpu.VMEM((LEAD + count, cap), BF16),
            pltpu.VMEM((3, LEAD + count, LANES), BF16),
            pltpu.VMEM((6, count, LANES), F32),
            pltpu.VMEM((3, LEAD + count, LANES), F32),
        ],
    )(drift, lengths, raw, tail, head, short, span, cot)


def medium_kernel(
    medium_ref,
    span_ref,
    cot_ref,
    filtered_ref,
    mixed_ref,
    mixed_halo_ref,
    weighted_ref,
    weighted_halo_ref,
    grad_ref,
    corr_ref,
    fore_rows,
    back_rows,
    fore_mask,
    back_mask,
    back_mask32,
):
    block = pl.program_id(0)
    taps = medium_ref.shape[0]

    @pl.when(block == 0)
    def _():
        source = iota((taps, LANES), 0)
        lane = iota((taps, LANES), 1)
        filt = medium_ref[...].astype(BF16)
        across = lambda pick: lax.dot_general(
            filt, pick, (((0,), (0,)), ((), ())), preferred_element_type=F32
        )
        fore_rows[...] = across(ones_where(lane == taps - source))
        back_rows[...] = across(ones_where(lane == source))
        before, after = column_of(span_ref[0:1]), column_of(span_ref[1:2])
        row = iota((HALF, LANES), 0)
        lane = iota((HALF, LANES), 1)
        for half in range(2):
            part = slice(HALF * half, HALF * half + HALF)
            lag = row + HALF - lane
            fore_mask[half] = ones_where((lag >= 0) & (lag < taps) & (lag <= before[part]))
            lag = lane - row
            back = (lag >= 0) & (lag < taps) & (lag <= after[part])
            back_mask[half] = ones_where(back)
            back_mask32[half] = ones_where(back, F32)

    fore = fore_rows[pl.ds(pl.multiple_of(block * 8, 8), 8)]
    back = back_rows[pl.ds(pl.multiple_of(block * 8, 8), 8)]
    toeplitz = lambda rows, g: pltpu.roll(
        jnp.broadcast_to(rows[g : g + 1], (HALF, LANES)).astype(BF16), 0, 1, stride=1, stride_axis=0
    )
    fores = [toeplitz(fore, g) for g in range(8)]
    backs = [toeplitz(back, g) for g in range(8)]
    group_of = iota((HALF, LANES), 1) // 16
    mixed = mixed_ref[...]
    weighted = weighted_ref[...]
    mixed_ext = jnp.concatenate([mixed_halo_ref[...], mixed], axis=0)
    weighted_ext = jnp.concatenate([weighted, weighted_halo_ref[...]], axis=0)
    corr = [None] * 8
    for half in range(2):
        part = slice(HALF * half, HALF * half + HALF)
        window = slice(HALF * half, HALF * half + 2 * HALF)
        mask = fore_mask[half]
        bands = jnp.concatenate([f * mask for f in fores], axis=0)
        every = dot(bands, mixed_ext[window])
        response = every[:HALF]
        for g in range(1, 8):
            response = jnp.where(group_of == g, every[HALF * g : HALF * g + HALF], response)
        mask = back_mask[half]
        bands = jnp.concatenate([b * mask for b in backs], axis=0)
        every = dot(bands, weighted_ext[window])
        spread = every[:HALF]
        for g in range(1, 8):
            spread = jnp.where(group_of == g, every[HALF * g : HALF * g + HALF], spread)
        grad_ref[0, part] = (cot_ref[part].astype(F32) * response).astype(BF16)
        grad_ref[1, part] = (spread * filtered_ref[1, part]).astype(BF16)
        grad_ref[2, part] = (spread * filtered_ref[0, part]).astype(BF16)
        zero = jnp.zeros((HALF, LANES), BF16)
        alone = jnp.concatenate(
            [jnp.where(group_of == g, mixed[part], zero) for g in range(8)], axis=0
        )
        every = dot_rows(alone, weighted_ext[window])
        for g in range(8):
            term = every[HALF * g : HALF * g + HALF] * back_mask32[half]
            corr[g] = term if half == 0 else corr[g] + term
    for g in range(8):
        total = corr[g][0:8]
        for strip in range(1, 8):
            total = total + pltpu.roll(corr[g][8 * strip : 8 * strip + 8], LANES - 8 * strip, 1)
        corr_ref[g] = total


def medium(filt, span, cot, filtered, mixed, mixed_halo, weighted, weighted_halo):
    taps, groups = filt.shape
    count, width = mixed.shape
    by_lane = lambda *lead: pl.BlockSpec(lead + (LANES,), lambda i: (0,) * len(lead) + (i,))
    whole = lambda a: pl.BlockSpec(a.shape, lambda i: (0,) * a.ndim)
    return pl.pallas_call(
        medium_kernel,
        grid=(width // LANES,),
        in_specs=[
            whole(filt),
            whole(span),
            by_lane(count),
            by_lane(2, count),
            by_lane(count),
            by_lane(HALF),
            by_lane(count),
            by_lane(HALF),
        ],
        out_specs=[
            by_lane(3, count),
            pl.BlockSpec((8, 8, LANES), lambda i: (i, 0, 0)),
        ],
        out_shape=[
            jax.ShapeDtypeStruct((3, count, width), BF16),
            jax.ShapeDtypeStruct((groups, 8, LANES), F32),
        ],
        scratch_shapes=[
            pltpu.VMEM((groups, LANES), F32),
            pltpu.VMEM((groups, LANES), F32),
            pltpu.VMEM((2, HALF, LANES), BF16),
            pltpu.VMEM((2, HALF, LANES), BF16),
            pltpu.VMEM((2, HALF, LANES), F32),
        ],
    )(filt, span, cot, filtered, mixed, mixed_halo, weighted, weighted_halo)


def backward_kernel(
    short_ref, span_ref, packed_ref, grad_ref, grad_halo_ref, corr_ref, out_ref, sums_ref, masks, rows
):
    block = pl.program_id(0)
    count = packed_ref.shape[1]
    groups = short_ref.shape[2]

    @pl.when(block == 0)
    def _():
        after = column_of(span_ref[1:2])
        for lag in range(1, 7):
            masks[lag - 1] = ones_where(after >= lag, F32)
        sums_ref[0:24] = jnp.zeros((24, groups), F32)
        taps = 64
        total = None
        for row in range(8):
            strip = corr_ref[:, row, :]
            strip = strip if row == 0 else pltpu.roll(strip, LANES - row, 1)
            total = strip if total is None else total + strip
        sums_ref[24 : 24 + taps] = jnp.transpose(total)[:taps]

    taps = widened_taps(short_ref, block, LANES)
    sums = []
    for part in range(3):
        rows[part, 0:count] = grad_ref[part].astype(F32)
        rows[part, count : count + 16] = grad_halo_ref[part].astype(F32)
        packed = packed_ref[part].astype(F32)
        total = None
        for lag in range(7):
            window = rows[part, lag : lag + count]
            if lag:
                window = masks[lag - 1] * window
            term = taps[part][lag : lag + 1] * window
            total = term if total is None else total + term
            sums.append(jnp.sum(packed * window, axis=0, keepdims=True))
        out_ref[part] = jnp.transpose(total).astype(BF16)
    sums = jnp.concatenate(sums + [jnp.zeros((3, LANES), F32)], axis=0)
    high = sums.astype(BF16)
    low = (sums - high.astype(F32)).astype(BF16)
    gather = ones_where(
        iota((LANES, groups), 1) == (block * LANES + iota((LANES, groups), 0)) // 16
    )
    sums_ref[0:24] = sums_ref[0:24] + dot(high, gather) + dot(low, gather)


def backward(short, span, packed, grad, grad_halo, corr):
    count, width = packed.shape[1:]
    groups = short.shape[2]
    by_lane = lambda *lead: pl.BlockSpec(lead + (LANES,), lambda i: (0,) * len(lead) + (i,))
    whole = lambda a: pl.BlockSpec(a.shape, lambda i: (0,) * a.ndim)
    return pl.pallas_call(
        backward_kernel,
        grid=(width // LANES,),
        in_specs=[
            whole(short),
            whole(span),
            by_lane(3, count),
            by_lane(3, count),
            by_lane(3, 16),
            whole(corr),
        ],
        out_specs=[
            pl.BlockSpec((3, LANES, count), lambda i: (0, i, 0)),
            pl.BlockSpec((88, groups), lambda i: (0, 0)),
        ],
        out_shape=[
            jax.ShapeDtypeStruct((3, width, count), BF16),
            jax.ShapeDtypeStruct((88, groups), F32),
        ],
        scratch_shapes=[
            pltpu.VMEM((6, count, LANES), F32),
            pltpu.VMEM((3, count + 16, LANES), F32),
        ],
    )(short, span, packed, grad, grad_halo, corr)


def total_kernel(scale, part_ref, short_out, medium_out, mine, first, second, result, send, sem1, sem2, sem3):
    x, ctx = lax.axis_index("dp"), lax.axis_index("ctx")
    z, yc = lax.div(ctx, 8), lax.rem(ctx, 8)
    y, core = lax.div(yc, 2), lax.rem(yc, 2)
    place1 = z * 2 + core
    place2 = x * 4 + y

    def peer1(other):
        return {"dp": x, "ctx": lax.div(other, 2) * 8 + y * 2 + lax.rem(other, 2)}

    def peer2(other):
        return {"dp": lax.div(other, 4), "ctx": z * 8 + lax.rem(other, 4) * 2 + core}

    barrier = pltpu.get_barrier_semaphore()
    for hop in range(1, 16):
        pl.semaphore_signal(
            barrier, inc=1, device_id=peer1(lax.rem(place1 + hop, 16)), device_id_type=MESH
        )
        pl.semaphore_signal(
            barrier, inc=1, device_id=peer2(lax.rem(place2 + hop, 16)), device_id_type=MESH
        )
    groups = part_ref.shape[1]
    for piece in range(11):
        mine[piece] = part_ref[8 * piece : 8 * piece + 8]
    for piece in range(11, 16):
        mine[piece] = jnp.zeros((8, groups), F32)
    pl.semaphore_wait(barrier, 30)

    def exchange(source, target, sems, peer, place):
        copies = []
        for hop in range(1, 16):
            other = lax.rem(place + hop, 16)
            copy = pltpu.make_async_remote_copy(
                source(other),
                target(hop),
                send.at[hop],
                sems.at[16 - hop],
                device_id=peer(other),
                device_id_type=MESH,
            )
            copy.start()
            copies.append(copy)
        for copy in copies:
            copy.wait()

    exchange(lambda other: mine.at[other], lambda hop: first.at[16 - hop], sem1, peer1, place1)
    total = mine[place1]
    for hop in range(1, 16):
        total = total + first[hop]
    second[0] = total
    exchange(lambda other: second.at[0], lambda hop: second.at[16 - hop], sem2, peer2, place2)
    total = jnp.zeros((8, groups), F32)
    for other in range(16):
        total = total + second[lax.rem(other - place2 + 16, 16)]
    result[place1] = total * (1.0 / scale)
    exchange(lambda other: result.at[place1], lambda hop: result.at[place1], sem3, peer1, place1)
    short_out[...] = jnp.concatenate([result[piece] for piece in range(3)], axis=0)
    for piece in range(3, 11):
        medium_out[8 * (piece - 3) : 8 * (piece - 3) + 8] = result[piece]


def total_over_devices(part, scale):
    groups = part.shape[1]
    vmem = pl.BlockSpec(memory_space=pltpu.VMEM)
    dma = pltpu.SemaphoreType.DMA((16,))
    return pl.pallas_call(
        functools.partial(total_kernel, scale),
        in_specs=[vmem],
        out_specs=[vmem, vmem],
        out_shape=[
            jax.ShapeDtypeStruct((24, groups), F32),
            jax.ShapeDtypeStruct((64, groups), F32),
        ],
        scratch_shapes=[
            pltpu.VMEM((16, 8, groups), F32),
            pltpu.VMEM((16, 8, groups), F32),
            pltpu.VMEM((16, 8, groups), F32),
            pltpu.VMEM((16, 8, groups), F32),
            dma,
            dma,
            dma,
            dma,
        ],
        compiler_params=pltpu.CompilerParams(collective_id=1, has_side_effects=True),
    )(part)


def passed_along(block, distance):
    devices = range(lax.axis_size("ctx"))
    route = [(i - distance, i) for i in devices if i - distance in devices]
    return lax.ppermute(block, "ctx", route)


def shards(raw_qkv, block_lengths, short_filter, medium_filter, doc_span, cotangent):
    count = cotangent.shape[2]
    groups = medium_filter.shape[0]
    group_size = cotangent.shape[1] // groups
    raw = jnp.transpose(raw_qkv[0], (0, 2, 1))
    lengths = block_lengths[0]
    short = jnp.pad(jnp.transpose(short_filter, (0, 2, 1)), ((0, 0), (0, 1), (0, 0)))
    filt = jnp.transpose(medium_filter)
    span = doc_span[0]
    cot = cotangent[0]

    tail = passed_along(build_tail(lengths, raw), 1)
    head = passed_along(raw[:, :HEAD_ROWS], -1)
    start = block_start(lengths)[0:1, 0:1]
    drift = start - lax.axis_index("ctx") * count
    packed, cot_rows, filtered, mixed, weighted = forward(
        drift, lengths, raw, tail, head, short, span, cot
    )
    mixed_halo = passed_along(mixed[count - HALF :], 1)
    weighted_halo = passed_along(weighted[:HALF], -1)
    grad, corr = medium(filt, span, cot_rows, filtered, mixed, mixed_halo, weighted, weighted_halo)
    grad_halo = passed_along(grad[:, :16], -1)
    out, sums = backward(short, span, packed, grad, grad_halo, corr)
    scale = math.sqrt(lax.axis_size("dp") * lax.axis_size("ctx") * count * group_size)
    short_sum, medium_sum = total_over_devices(sums, scale)
    short_grad = jnp.transpose(short_sum[:21].reshape(3, 7, groups), (0, 2, 1))
    return (out[None], short_grad, jnp.transpose(medium_sum))


def solution(mesh):
    return jax.shard_map(
        shards,
        mesh=mesh,
        in_specs=(
            P("dp", None, None, "ctx"),
            P("dp", "ctx", None),
            P(),
            P(),
            P("dp", None, "ctx"),
            P("dp", None, "ctx"),
        ),
        out_specs=(P("dp", None, None, "ctx"), P(), P()),
        check_vma=False,
    )
```

```python
import functools
import math
import types

import jax
import jax.numpy as jnp
from jax import lax
from jax.experimental import pallas as pl
from jax.experimental.pallas import tpu as pltpu
from jax.sharding import PartitionSpec as P

F32 = jnp.float32
BF16 = jnp.bfloat16
I32 = jnp.int32
MESH = pl.DeviceIdType.MESH
LANES = 128
WIDE = 256
REACH = 22
TAIL_ROWS = 80
HEAD_ROWS = 16
LEAD = 8
HALF = 64
COUNT = 128
TEAM = 16
INNER = 8


def iota(shape, dim):
    return lax.broadcasted_iota(I32, shape, dim)


def ones_where(condition, dtype=BF16):
    return jnp.where(condition, 1.0, 0.0).astype(dtype)


def dot(left, right):
    return jnp.dot(left, right, preferred_element_type=F32)


def dot_rows(left, right):
    return lax.dot_general(left, right, (((1,), (1,)), ((), ())), preferred_element_type=F32)


def dot_columns(left, right):
    return lax.dot_general(left, right, (((0,), (0,)), ((), ())), preferred_element_type=F32)


def column_of(row):
    return jnp.transpose(jnp.broadcast_to(row, (LANES, LANES)))


def halves():
    return [slice(LANES * side, LANES * side + LANES) for side in range(WIDE // LANES)]


def build_tables(r):
    before, after = column_of(r.span[0:1]), column_of(r.span[1:2])
    for lag in range(1, 7):
        r.fore_short[lag - 1] = ones_where(before >= lag, F32)
        r.back_short[lag - 1] = ones_where(after >= lag, F32)
    taps = r.medium.shape[0]
    source = iota((taps, LANES), 0)
    lane = iota((taps, LANES), 1)
    filt = r.medium[...].astype(BF16)
    r.fore_rows[...] = dot_columns(filt, ones_where(lane == taps - source))
    r.back_rows[...] = dot_columns(filt, ones_where(lane == source))
    row = iota((HALF, LANES), 0)
    lane = iota((HALF, LANES), 1)
    for half in range(2):
        part = slice(HALF * half, HALF * half + HALF)
        lag = row + HALF - lane
        r.fore_mask[half] = ones_where((lag >= 0) & (lag < taps) & (lag <= before[part]))
        lag = lane - row
        back = (lag >= 0) & (lag < taps) & (lag <= after[part])
        r.back_mask[half] = ones_where(back)
        r.back_mask32[half] = ones_where(back, F32)
    live = r.lengths[0, 0] + r.lengths[0, 1]
    place = iota((TAIL_ROWS, r.cap), 0)
    column = iota((TAIL_ROWS, r.cap), 1)
    for part in range(3):
        step = place - REACH * part
        pick = (step >= 0) & (step < REACH) & (column == live - REACH + step)
        r.tail_pick[part] = ones_where(pick)


def widen_taps(r, chunk):
    groups = r.short.shape[2]
    owner = (chunk * WIDE + iota((groups, WIDE), 1)) // 16
    spread = ones_where(iota((groups, WIDE), 0) == owner)
    for part in range(3):
        r.taps[chunk, part, 0:7] = dot(r.short[part].astype(BF16), spread)


def tail_chunk(r, chunk):
    total = dot(r.tail_pick[0], r.raw[chunk, 0])
    for part in range(1, 3):
        total = total + dot(r.tail_pick[part], r.raw[chunk, part])
    r.tail_out[chunk] = total.astype(BF16).reshape(TAIL_ROWS // 16, 16, WIDE)


def build_picks(r, drift):
    live = r.lengths[0, 0] + r.lengths[0, 1]
    shape = (LEAD + COUNT, r.cap)
    token = iota(shape, 0) - LEAD - jnp.broadcast_to(drift, shape)
    column = iota(shape, 1)
    r.own_pick[...] = ones_where((column == token) & (column < live))
    shape = (LEAD + COUNT, LANES)
    token = iota(shape, 0) - LEAD - jnp.broadcast_to(drift, shape)
    column = iota(shape, 1)
    for part in range(3):
        late = token + REACH
        from_tail = (late >= 0) & (late < REACH) & (column == REACH * part + late)
        over = token - live
        from_head = (over >= 0) & (column == TAIL_ROWS + HEAD_ROWS * part + over)
        r.edge_pick[part] = ones_where(from_tail | from_head)


def strips(rows):
    return [slice(first, first + rows) for first in range(0, COUNT, rows)]


def filter_strip(r, chunk, part, lanes, window, masks):
    total = r.taps[chunk, part, 0:1, lanes] * window(0)
    for lag in range(1, 7):
        total = total + r.taps[chunk, part, lag : lag + 1, lanes] * (masks[lag - 1] * window(lag))
    return total


def forward_chunk(r, chunk):
    edges = r.edges[chunk].reshape(COUNT, WIDE)
    for part in range(3):
        packed = dot(r.own_pick[...], r.raw[chunk, part]) + dot(r.edge_pick[part], edges)
        for side, lanes in enumerate(halves()):
            r.rows[chunk, part, side] = packed[:, lanes]
    for side, lanes in enumerate(halves()):
        cot = jnp.transpose(r.cot[chunk, lanes].astype(F32))
        r.cot_rows[chunk, :, lanes] = cot
        for strip in strips(32):
            masks = [r.fore_short[lag, strip] for lag in range(6)]
            query, key, value = [
                filter_strip(
                    r,
                    chunk,
                    part,
                    lanes,
                    lambda lag: r.rows[chunk, part, side, LEAD + strip.start - lag : LEAD + strip.stop - lag],
                    masks,
                )
                for part in range(3)
            ]
            r.filtered[chunk, 0, strip, lanes] = key
            r.filtered[chunk, 1, strip, lanes] = value
            r.mixed[chunk, HALF + strip.start : HALF + strip.stop, lanes] = (key * value).astype(BF16)
            r.weighted[chunk, strip, lanes] = (cot[strip] * query).astype(BF16)


def toeplitz(rows, g):
    row = jnp.broadcast_to(rows[g : g + 1], (HALF, LANES)).astype(BF16)
    return pltpu.roll(row, 0, 1, stride=1, stride_axis=0)


def own_lanes(every, pair_of):
    result = every[:HALF]
    for pair in range(1, 4):
        result = jnp.where(pair_of == pair, every[HALF * pair : HALF * pair + HALF], result)
    return result


def paired(bands, mask):
    bands = [band * mask for band in bands]
    pairs = [jnp.concatenate(bands[2 * p : 2 * p + 2], axis=1) for p in range(4)]
    return jnp.concatenate(pairs, axis=0)


def medium_chunk(r, chunk):
    shape = (HALF + COUNT, LANES)
    even = iota(shape, 1) // 16 % 2 == 0
    pair_of = iota((HALF, LANES), 1) // 32
    for side, lanes in enumerate(halves()):
        first = pl.multiple_of(chunk * 16 + 8 * side, 8)
        fore = r.fore_rows[pl.ds(first, 8)]
        back = r.back_rows[pl.ds(first, 8)]
        fores = [toeplitz(fore, g) for g in range(8)]
        backs = [toeplitz(back, g) for g in range(8)]
        mixed = r.mixed[chunk, :, lanes]
        weighted = r.weighted[chunk, :, lanes]
        zero = jnp.zeros(shape, BF16)
        mixed_of = [jnp.where(even, mixed, zero), jnp.where(even, zero, mixed)]
        weighted_of = [jnp.where(even, weighted, zero), jnp.where(even, zero, weighted)]
        corr = [None] * 8
        for half in range(2):
            part = slice(HALF * half, HALF * half + HALF)
            window = slice(HALF * half, HALF * half + 2 * HALF)
            earlier = jnp.concatenate([m[window] for m in mixed_of], axis=0)
            later = jnp.concatenate([w[window] for w in weighted_of], axis=0)
            response = own_lanes(dot(paired(fores, r.fore_mask[half]), earlier), pair_of)
            spread = own_lanes(dot(paired(backs, r.back_mask[half]), later), pair_of)
            grads = (
                r.cot_rows[chunk, part, lanes] * response,
                spread * r.filtered[chunk, 1, part, lanes],
                spread * r.filtered[chunk, 0, part, lanes],
            )
            for b in range(3):
                grad = grads[b].astype(BF16)
                if half == 0:
                    r.grad_head[chunk, b, :, lanes] = grad[:HEAD_ROWS]
                r.grads[chunk, b, side, part] = grad.astype(F32)
            own = mixed[HALF + HALF * half : 2 * HALF + HALF * half]
            alone = [jnp.where(pair_of == p, own, zero[:HALF]) for p in range(4)]
            every = dot_rows(jnp.concatenate(alone, axis=0), later)
            mask = r.back_mask32[half]
            for g in range(8):
                tile = every[HALF * (g // 2) : HALF * (g // 2) + HALF]
                term = tile[:, LANES * (g % 2) : LANES * (g % 2) + LANES] * mask
                corr[g] = term if half == 0 else corr[g] + term
        for g in range(8):
            total = corr[g][0:8]
            for strip in range(1, 8):
                total = total + pltpu.roll(corr[g][8 * strip : 8 * strip + 8], LANES - 8 * strip, 1)
            r.corr[first + g] = total


def medium_sums(r):
    total = None
    for row in range(8):
        strip = r.corr[:, row, :]
        strip = strip if row == 0 else pltpu.roll(strip, LANES - row, 1)
        total = strip if total is None else total + strip
    total = jnp.transpose(total)
    for place in range(TEAM):
        strip, side = place // 2, place % 2
        r.sum_mine[place, 0:8] = total[8 * strip : 8 * strip + 8, LANES * side : LANES * side + LANES]


def short_sums_chunk(r, chunk):
    for side, lanes in enumerate(halves()):
        sums = [None] * 24
        for strip in strips(16):
            masks = [r.fore_short[lag, strip] for lag in range(6)]
            for part in range(3):
                grad = r.grads[chunk, part, side, strip]
                for lag in range(7):
                    window = r.rows[chunk, part, side, LEAD + strip.start - lag : LEAD + strip.stop - lag]
                    term = grad * window if lag == 0 else (masks[lag - 1] * grad) * window
                    term = term[0:8] + term[8:16]
                    place = 7 * part + lag
                    sums[place] = term if sums[place] is None else sums[place] + term
        for place in range(21):
            r.short_parts[(chunk * 2 + side) * 24 + place] = sums[place]


def short_sums(r):
    total = r.short_parts[:, 0, :]
    for row in range(1, 8):
        total = total + r.short_parts[:, row, :]
    gather = ones_where(iota((LANES, LANES), 1) == iota((LANES, LANES), 0) // 16)
    high = total.astype(BF16)
    low = (total - high.astype(F32)).astype(BF16)
    grouped = dot(high, gather) + dot(low, gather)
    for side in range(2):
        total = None
        for block in range(16):
            first = (16 * side + block) * 24
            strip = grouped[first : first + 24]
            strip = pltpu.roll(strip, 8 * block, 1) if block else strip
            total = strip if total is None else total + strip
        for place in range(side, TEAM, 2):
            r.sum_mine[place, 8:11] = total[3 * (place // 2) : 3 * (place // 2) + 3]


def backward_chunk(r, chunk):
    for side, lanes in enumerate(halves()):
        totals = [[], [], []]
        for part in range(3):
            r.grads[chunk, part, side, COUNT:] = r.grad_halo[chunk, part, :, lanes].astype(F32)
        for strip in strips(32):
            masks = [r.back_short[lag, strip] for lag in range(6)]
            for part in range(3):
                window = lambda lag: r.grads[chunk, part, side, strip.start + lag : strip.stop + lag]
                totals[part].append(filter_strip(r, chunk, part, lanes, window, masks))
        rows = pl.ds(pl.multiple_of(chunk * WIDE + LANES * side, LANES), LANES)
        for part in range(3):
            r.out[part, rows] = jnp.transpose(jnp.concatenate(totals[part], axis=0)).astype(BF16)


OPERANDS = ["lengths", "raw_hbm", "short", "medium", "span", "cot_hbm"]
RESULTS = ["out", "short_out", "medium_out"]


def scratch(cap, chunks, groups):
    vmem = pltpu.VMEM
    dma = pltpu.SemaphoreType.DMA
    return {
        "raw": vmem((chunks, 3, cap, WIDE), BF16),
        "cot": vmem((chunks, WIDE, COUNT), BF16),
        "tail_out": vmem((chunks, TAIL_ROWS // 16, 16, WIDE), BF16),
        "edges": vmem((chunks, 8, 16, WIDE), BF16),
        "own_pick": vmem((LEAD + COUNT, cap), BF16),
        "edge_pick": vmem((3, LEAD + COUNT, LANES), BF16),
        "tail_pick": vmem((3, TAIL_ROWS, cap), BF16),
        "fore_short": vmem((6, COUNT, LANES), F32),
        "back_short": vmem((6, COUNT, LANES), F32),
        "taps": vmem((chunks, 3, 8, WIDE), F32),
        "rows": vmem((chunks, 3, 2, LEAD + COUNT, LANES), F32),
        "filtered": vmem((chunks, 2, COUNT, WIDE), F32),
        "cot_rows": vmem((chunks, COUNT, WIDE), F32),
        "mixed": vmem((chunks, HALF + COUNT, WIDE), BF16),
        "weighted": vmem((chunks, COUNT + HALF, WIDE), BF16),
        "fore_rows": vmem((groups, LANES), F32),
        "back_rows": vmem((groups, LANES), F32),
        "fore_mask": vmem((2, HALF, LANES), BF16),
        "back_mask": vmem((2, HALF, LANES), BF16),
        "back_mask32": vmem((2, HALF, LANES), F32),
        "grads": vmem((chunks, 3, 2, COUNT + 16, LANES), F32),
        "grad_head": vmem((chunks, 3, HEAD_ROWS, WIDE), BF16),
        "grad_halo": vmem((chunks, 3, HEAD_ROWS, WIDE), BF16),
        "corr": vmem((groups, 8, LANES), F32),
        "short_parts": vmem((chunks * 2 * 24, 8, LANES), F32),
        "live_out": vmem((2, 8, LANES), I32),
        "live_near": vmem((INNER, 8, LANES), I32),
        "live_far": vmem((INNER, 8, LANES), I32),
        "sum_mine": vmem((TEAM, 11, LANES), F32),
        "sum_first": vmem((TEAM, 11, LANES), F32),
        "sum_second": vmem((TEAM, 11, LANES), F32),
        "sum_all": vmem((TEAM, 11, LANES), F32),
        "short_all": vmem((24, groups), F32),
        "load_sem": dma((2, chunks)),
        "send_sem": dma((5, chunks)),
        "recv_sem": dma((5, chunks)),
        "live_send": dma((2, INNER)),
        "live_recv": dma((2, INNER)),
        "sum_send": dma((3, TEAM)),
        "sum_recv": dma((3, TEAM)),
    }


def kernel(names, scale, *refs):
    r = types.SimpleNamespace(**dict(zip(names, refs)))
    r.cap = r.raw.shape[2]
    chunks = r.raw.shape[0]
    x, me = lax.axis_index("dp"), lax.axis_index("ctx")
    dp_count, ctx_count = lax.axis_size("dp"), lax.axis_size("ctx")
    right, left = lax.rem(me + 1, ctx_count), lax.rem(me + ctx_count - 1, ctx_count)
    row, col = lax.div(me, INNER), lax.rem(me, INNER)
    y, core = lax.div(col, 2), lax.rem(col, 2)
    place1, place2 = row * 2 + core, x * 4 + y

    def near_peer(hop):
        return {"ctx": row * INNER + lax.rem(col + hop, INNER)}

    def far_peer(hop):
        return {"ctx": lax.rem(row + hop, INNER) * INNER + col}

    def peer1(other):
        return {"dp": x, "ctx": lax.div(other, 2) * INNER + y * 2 + lax.rem(other, 2)}

    def peer2(other):
        return {"dp": lax.div(other, 4), "ctx": row * INNER + lax.rem(other, 4) * 2 + core}

    def remote(src, dst, send, recv, device):
        return pltpu.make_async_remote_copy(
            src, dst, send, recv, device_id=device, device_id_type=MESH
        )

    def load_raw(c):
        lanes = pl.ds(pl.multiple_of(c * WIDE, WIDE), WIDE)
        return pltpu.make_async_copy(r.raw_hbm.at[:, :, lanes], r.raw.at[c], r.load_sem.at[0, c])

    def load_cot(c):
        rows = pl.ds(pl.multiple_of(c * WIDE, WIDE), WIDE)
        return pltpu.make_async_copy(r.cot_hbm.at[rows], r.cot.at[c], r.load_sem.at[1, c])

    def send_tail(c):
        dst = r.edges.at[c, 0 : TAIL_ROWS // 16]
        return remote(r.tail_out.at[c], dst, r.send_sem.at[0, c], r.recv_sem.at[0, c], {"ctx": right})

    def send_head(c):
        src, dst = r.raw.at[c, :, 0:HEAD_ROWS], r.edges.at[c, TAIL_ROWS // 16 : 8]
        return remote(src, dst, r.send_sem.at[1, c], r.recv_sem.at[1, c], {"ctx": left})

    def send_mixed(c):
        src, dst = r.mixed.at[c, COUNT : COUNT + HALF], r.mixed.at[c, 0:HALF]
        return remote(src, dst, r.send_sem.at[2, c], r.recv_sem.at[2, c], {"ctx": right})

    def send_weighted(c):
        src, dst = r.weighted.at[c, 0:HALF], r.weighted.at[c, COUNT : COUNT + HALF]
        return remote(src, dst, r.send_sem.at[3, c], r.recv_sem.at[3, c], {"ctx": left})

    def send_grad(c):
        src, dst = r.grad_head.at[c], r.grad_halo.at[c]
        return remote(src, dst, r.send_sem.at[4, c], r.recv_sem.at[4, c], {"ctx": left})

    def live_copies(stage):
        near = stage == 0
        inbox = r.live_near if near else r.live_far
        return [
            remote(
                r.live_out.at[stage],
                inbox.at[INNER - hop],
                r.live_send.at[stage, hop],
                r.live_recv.at[stage, INNER - hop],
                near_peer(hop) if near else far_peer(hop),
            )
            for hop in range(1, INNER)
        ]

    def sum_copies(stage, source, target, peer, place):
        copies = []
        for hop in range(1, TEAM):
            other = lax.rem(place + hop, TEAM)
            copies.append(
                remote(
                    source(other),
                    target(TEAM - hop),
                    r.sum_send.at[stage, hop],
                    r.sum_recv.at[stage, TEAM - hop],
                    peer(other),
                )
            )
        return copies

    def start(copies):
        for copy in copies:
            copy.start()

    def finish(copies):
        for copy in copies:
            copy.wait()

    def each(step, first=0, last=chunks):
        def body(c, carry):
            step(c)
            return carry

        lax.fori_loop(first, last, body, 0)

    barrier = pltpu.get_barrier_semaphore()
    peers = [{"ctx": right}, {"ctx": left}]
    peers += [near_peer(hop) for hop in range(1, INNER)]
    peers += [far_peer(hop) for hop in range(1, INNER)]
    peers += [{"dp": lax.rem(x + hop, dp_count)} for hop in range(1, dp_count)]

    def loads(c):
        load_raw(c).start()

    each(loads)
    for peer in peers:
        pl.semaphore_signal(barrier, inc=1, device_id=peer, device_id_type=MESH)

    def cot_loads(c):
        load_cot(c).start()

    each(cot_loads)
    live = r.lengths[0, 0] + r.lengths[0, 1]
    r.live_out[0] = jnp.zeros((8, LANES), I32) + live
    build_tables(r)

    def tails(c):
        load_raw(c).wait()
        tail_chunk(r, c)

    each(tails, 0, chunks // 2)
    pl.semaphore_wait(barrier, len(peers))
    near = live_copies(0)
    start(near)

    def edges(c):
        send_tail(c).start()
        send_head(c).start()

    each(edges, 0, chunks // 2)
    finish(near)
    ahead = jnp.zeros((8, LANES), I32)
    whole = r.live_out[0]
    for hop in range(1, INNER):
        value = r.live_near[hop]
        whole = whole + value
        ahead = ahead + value * jnp.where(col + hop >= INNER, 1, 0)
    r.live_out[1] = whole
    far = live_copies(1)
    start(far)

    def tails_edges(c):
        tails(c)
        edges(c)

    each(tails_edges, chunks // 2, chunks)

    def widen(c):
        widen_taps(r, c)
        load_cot(c).wait()

    each(widen)
    finish(far)
    for hop in range(1, INNER):
        ahead = ahead + r.live_far[hop] * jnp.where(row + hop >= INNER, 1, 0)
    build_picks(r, ahead[0:1, 0:1] - me * COUNT)

    def forward(c):
        send_tail(c).wait_recv()
        send_head(c).wait_recv()
        forward_chunk(r, c)
        send_mixed(c).start()
        send_weighted(c).start()

    each(forward)

    def medium(c):
        send_mixed(c).wait_recv()
        send_weighted(c).wait_recv()
        medium_chunk(r, c)
        send_grad(c).start()
        short_sums_chunk(r, c)

    each(medium)
    medium_sums(r)
    short_sums(r)
    spread_out = sum_copies(
        0, lambda o: r.sum_mine.at[o], lambda h: r.sum_first.at[h], peer1, place1
    )
    start(spread_out)

    def backward(c):
        send_grad(c).wait_recv()
        backward_chunk(r, c)

    each(backward, 0, chunks * 3 // 8)
    finish(spread_out)
    total = r.sum_mine[place1]
    for hop in range(1, TEAM):
        total = total + r.sum_first[hop]
    r.sum_second[0] = total
    across = sum_copies(
        1, lambda o: r.sum_second.at[0], lambda h: r.sum_second.at[h], peer2, place2
    )
    start(across)
    each(backward, chunks * 3 // 8, chunks * 3 // 4)
    finish(across)
    total = jnp.zeros((11, LANES), F32)
    for other in range(TEAM):
        total = total + r.sum_second[lax.rem(other - place2 + TEAM, TEAM)]
    r.sum_all[place1] = total * (1.0 / scale)
    handed = sum_copies(
        2, lambda o: r.sum_all.at[place1], lambda h: r.sum_all.at[place1], peer1, place1
    )
    start(handed)
    each(backward, chunks * 3 // 4, chunks)
    finish(handed)
    for place in range(TEAM):
        strip, side = place // 2, place % 2
        lanes = slice(LANES * side, LANES * side + LANES)
        r.medium_out[8 * strip : 8 * strip + 8, lanes] = r.sum_all[place, 0:8]
        r.short_all[3 * strip : 3 * strip + 3, lanes] = r.sum_all[place, 8:11]
    for part in range(3):
        r.short_out[part] = r.short_all[7 * part : 7 * part + 7]

    def settle(c):
        for send in (send_tail, send_head, send_mixed, send_weighted, send_grad):
            send(c).wait_send()

    each(settle)


def shards(raw_qkv, block_lengths, short_filter, medium_filter, doc_span, cotangent):
    count = cotangent.shape[2]
    width = cotangent.shape[1]
    groups = medium_filter.shape[0]
    group_size = width // groups
    raw = jnp.transpose(raw_qkv[0], (0, 2, 1))
    short = jnp.transpose(short_filter, (0, 2, 1))
    filt = jnp.transpose(medium_filter)
    scale = math.sqrt(lax.axis_size("dp") * lax.axis_size("ctx") * count * group_size)
    space = scratch(raw.shape[1], width // WIDE, groups)
    vmem = pl.BlockSpec(memory_space=pltpu.VMEM)
    anywhere = pl.BlockSpec(memory_space=pl.ANY)
    out, short_sum, medium_sum = pl.pallas_call(
        functools.partial(kernel, OPERANDS + RESULTS + list(space), scale),
        in_specs=[pl.BlockSpec(memory_space=pltpu.SMEM), anywhere, vmem, vmem, vmem, anywhere],
        out_specs=[vmem, vmem, vmem],
        out_shape=[
            pltpu.VMEM((3, width, count), BF16),
            jax.ShapeDtypeStruct((3, 7, groups), F32),
            jax.ShapeDtypeStruct((64, groups), F32),
        ],
        scratch_shapes=list(space.values()),
        compiler_params=pltpu.CompilerParams(
            collective_id=0, has_side_effects=True, vmem_limit_bytes=56 * 1024 * 1024
        ),
    )(block_lengths[0], raw, short, filt, doc_span[0], cotangent[0])
    return (out[None], jnp.transpose(short_sum, (0, 2, 1)), jnp.transpose(medium_sum))


def solution(mesh):
    return jax.shard_map(
        shards,
        mesh=mesh,
        in_specs=(
            P("dp", None, None, "ctx"),
            P("dp", "ctx", None),
            P(),
            P(),
            P("dp", None, "ctx"),
            P("dp", None, "ctx"),
        ),
        out_specs=(P("dp", None, None, "ctx"), P(), P()),
        check_vma=False,
    )
```

```python
import functools
import math
import types

import jax
import jax.numpy as jnp
from jax import lax
from jax.experimental import pallas as pl
from jax.experimental.pallas import tpu as pltpu
from jax.sharding import PartitionSpec as P

F32 = jnp.float32
BF16 = jnp.bfloat16
I32 = jnp.int32
MESH = pl.DeviceIdType.MESH
LANES = 128
WIDE = 256
REACH = 22
TAIL_ROWS = 80
HEAD_ROWS = 16
LEAD = 8
HALF = 64
COUNT = 128
TEAM = 16
INNER = 8


def iota(shape, dim):
    return lax.broadcasted_iota(I32, shape, dim)


def ones_where(condition, dtype=BF16):
    return jnp.where(condition, 1.0, 0.0).astype(dtype)


def dot(left, right):
    return jnp.dot(left, right, preferred_element_type=F32)


def dot_columns(left, right):
    return lax.dot_general(left, right, (((0,), (0,)), ((), ())), preferred_element_type=F32)


def column_of(row):
    return jnp.transpose(jnp.broadcast_to(row, (LANES, LANES)))


def halves():
    return [slice(LANES * side, LANES * side + LANES) for side in range(WIDE // LANES)]


def build_tables(r):
    before, after = column_of(r.span[0:1]), column_of(r.span[1:2])
    for lag in range(1, 7):
        r.fore_short[lag - 1] = ones_where(before >= lag, F32)
        r.back_short[lag - 1] = ones_where(after >= lag, F32)
    taps = r.medium.shape[0]
    source = iota((taps, LANES), 0)
    lane = iota((taps, LANES), 1)
    filt = r.medium[...].astype(BF16)
    r.fore_rows[...] = dot_columns(filt, ones_where(lane == taps - source))
    r.back_rows[...] = dot_columns(filt, ones_where(lane == source))
    row = iota((HALF, LANES), 0)
    lane = iota((HALF, LANES), 1)
    for half in range(2):
        part = slice(HALF * half, HALF * half + HALF)
        lag = row + HALF - lane
        r.fore_mask[half] = ones_where((lag >= 0) & (lag < taps) & (lag <= before[part]))
        lag = lane - row
        back = (lag >= 0) & (lag < taps) & (lag <= after[part])
        r.back_mask[half] = ones_where(back)
        r.back_mask32[half] = ones_where(back, F32)
    live = r.lengths[0, 0] + r.lengths[0, 1]
    place = iota((TAIL_ROWS, r.cap), 0)
    column = iota((TAIL_ROWS, r.cap), 1)
    for part in range(3):
        step = place - REACH * part
        pick = (step >= 0) & (step < REACH) & (column == live - REACH + step)
        r.tail_pick[part] = ones_where(pick)


def widen_taps(r, chunk):
    span = LANES * 16 // WIDE
    owner = lax.rem(chunk, span) * (WIDE // 16) + iota((LANES, WIDE), 1) // 16
    spread = ones_where(iota((LANES, WIDE), 0) == owner)
    window = pl.ds(pl.multiple_of(lax.div(chunk, span) * LANES, LANES), LANES)
    for part in range(3):
        r.taps[chunk, part, 0:7] = dot(r.short[part, :, window].astype(BF16), spread)


def tail_chunk(r, chunk):
    total = dot(r.tail_pick[0], r.raw[chunk, 0])
    for part in range(1, 3):
        total = total + dot(r.tail_pick[part], r.raw[chunk, part])
    r.tail_out[chunk] = total.astype(BF16).reshape(TAIL_ROWS // 16, 16, WIDE)


def build_picks(r, drift):
    live = r.lengths[0, 0] + r.lengths[0, 1]
    shape = (LEAD + COUNT, r.cap)
    token = iota(shape, 0) - LEAD - jnp.broadcast_to(drift, shape)
    column = iota(shape, 1)
    r.own_pick[...] = ones_where((column == token) & (column < live))
    shape = (LEAD + COUNT, LANES)
    token = iota(shape, 0) - LEAD - jnp.broadcast_to(drift, shape)
    column = iota(shape, 1)
    for part in range(3):
        late = token + REACH
        from_tail = (late >= 0) & (late < REACH) & (column == REACH * part + late)
        over = token - live
        from_head = (over >= 0) & (column == TAIL_ROWS + HEAD_ROWS * part + over)
        r.edge_pick[part] = ones_where(from_tail | from_head)


def strips(rows):
    return [slice(first, first + rows) for first in range(0, COUNT, rows)]


def filter_strip(r, chunk, part, lanes, window, masks):
    total = r.taps[chunk, part, 0:1, lanes] * window(0)
    for lag in range(1, 7):
        total = total + r.taps[chunk, part, lag : lag + 1, lanes] * (masks[lag - 1] * window(lag))
    return total


def forward_chunk(r, chunk):
    edges = r.edges[chunk].reshape(COUNT, WIDE)
    for part in range(3):
        packed = dot(r.own_pick[...], r.raw[chunk, part]) + dot(r.edge_pick[part], edges)
        for side, lanes in enumerate(halves()):
            r.rows[chunk, part, side] = packed[:, lanes]
    for side, lanes in enumerate(halves()):
        cot = jnp.transpose(r.cot[chunk, lanes].astype(F32))
        r.cot_rows[chunk, :, lanes] = cot
        for strip in strips(32):
            masks = [r.fore_short[lag, strip] for lag in range(6)]
            query, key, value = [
                filter_strip(
                    r,
                    chunk,
                    part,
                    lanes,
                    lambda lag: r.rows[chunk, part, side, LEAD + strip.start - lag : LEAD + strip.stop - lag],
                    masks,
                )
                for part in range(3)
            ]
            r.filtered[chunk, 0, strip, lanes] = key
            r.filtered[chunk, 1, strip, lanes] = value
            r.mixed[chunk, HALF + strip.start : HALF + strip.stop, lanes] = (key * value).astype(BF16)
            r.weighted[chunk, strip, lanes] = (cot[strip] * query).astype(BF16)


def toeplitz(rows, g):
    row = jnp.broadcast_to(rows[g : g + 1], (HALF, LANES)).astype(BF16)
    return pltpu.roll(row, 0, 1, stride=1, stride_axis=0)


def own_lanes(every, pair_of):
    result = every[:HALF]
    for pair in range(1, 4):
        result = jnp.where(pair_of == pair, every[HALF * pair : HALF * pair + HALF], result)
    return result


def paired(bands, mask):
    bands = [band * mask for band in bands]
    pairs = [jnp.concatenate(bands[2 * p : 2 * p + 2], axis=1) for p in range(4)]
    return jnp.concatenate(pairs, axis=0)


def medium_chunk(r, chunk):
    shape = (HALF + COUNT, LANES)
    even = iota(shape, 1) // 16 % 2 == 0
    pair_of = iota((HALF, LANES), 1) // 32
    for side, lanes in enumerate(halves()):
        first = pl.multiple_of(chunk * 16 + 8 * side, 8)
        fore = r.fore_rows[pl.ds(first, 8)]
        back = r.back_rows[pl.ds(first, 8)]
        fores = [toeplitz(fore, g) for g in range(8)]
        backs = [toeplitz(back, g) for g in range(8)]
        mixed = r.mixed[chunk, :, lanes]
        weighted = r.weighted[chunk, :, lanes]
        zero = jnp.zeros(shape, BF16)
        mixed_of = [jnp.where(even, mixed, zero), jnp.where(even, zero, mixed)]
        weighted_of = [jnp.where(even, weighted, zero), jnp.where(even, zero, weighted)]
        corr = [None] * 8
        for half in range(2):
            part = slice(HALF * half, HALF * half + HALF)
            window = slice(HALF * half, HALF * half + 2 * HALF)
            earlier = jnp.concatenate([m[window] for m in mixed_of], axis=0)
            later = jnp.concatenate([w[window] for w in weighted_of], axis=0)
            response = own_lanes(dot(paired(fores, r.fore_mask[half]), earlier), pair_of)
            spread = own_lanes(dot(paired(backs, r.back_mask[half]), later), pair_of)
            grads = (
                r.cot_rows[chunk, part, lanes] * response,
                spread * r.filtered[chunk, 1, part, lanes],
                spread * r.filtered[chunk, 0, part, lanes],
            )
            for b in range(3):
                grad = grads[b].astype(BF16)
                if half == 0:
                    r.grad_head[chunk, b, :, lanes] = grad[:HEAD_ROWS]
                r.grads[chunk, b, side, part] = grad.astype(F32)
            own = mixed[HALF + HALF * half : 2 * HALF + HALF * half]
            alone = [jnp.where(pair_of == p, own, zero[:HALF]) for p in range(4)]
            turned = jnp.transpose(weighted[window])
            blank = jnp.zeros((16, LANES), BF16)
            sides = []
            for parity in range(2):
                blocks = [turned[16 * g : 16 * g + 16] if g % 2 == parity else blank for g in range(8)]
                sides.append(jnp.concatenate(blocks, axis=0))
            every = dot(jnp.concatenate(alone, axis=0), jnp.concatenate(sides, axis=1))
            mask = r.back_mask32[half]
            for g in range(8):
                tile = every[HALF * (g // 2) : HALF * (g // 2) + HALF]
                term = tile[:, LANES * (g % 2) : LANES * (g % 2) + LANES] * mask
                corr[g] = term if half == 0 else corr[g] + term
        for g in range(8):
            total = corr[g][0:8]
            for strip in range(1, 8):
                total = total + pltpu.roll(corr[g][8 * strip : 8 * strip + 8], LANES - 8 * strip, 1)
            r.corr[first + g] = total


def medium_sums(r):
    total = None
    for row in range(8):
        strip = r.corr[:, row, :]
        strip = strip if row == 0 else pltpu.roll(strip, LANES - row, 1)
        total = strip if total is None else total + strip
    total = jnp.transpose(total)
    for place in range(TEAM):
        strip, side = place // 2, place % 2
        r.sum_mine[place, 0:8] = total[8 * strip : 8 * strip + 8, LANES * side : LANES * side + LANES]


def short_sums_chunk(r, chunk):
    for side, lanes in enumerate(halves()):
        sums = [None] * 24
        for strip in strips(16):
            masks = [r.fore_short[lag, strip] for lag in range(6)]
            for part in range(3):
                grad = r.grads[chunk, part, side, strip]
                for lag in range(7):
                    window = r.rows[chunk, part, side, LEAD + strip.start - lag : LEAD + strip.stop - lag]
                    term = grad * window if lag == 0 else (masks[lag - 1] * grad) * window
                    term = term[0:8] + term[8:16]
                    place = 7 * part + lag
                    sums[place] = term if sums[place] is None else sums[place] + term
        for place in range(21):
            r.short_parts[(chunk * 2 + side) * 24 + place] = sums[place]


def short_sums(r):
    total = r.short_parts[:, 0, :]
    for row in range(1, 8):
        total = total + r.short_parts[:, row, :]
    gather = ones_where(iota((LANES, LANES), 1) == iota((LANES, LANES), 0) // 16)
    high = total.astype(BF16)
    low = (total - high.astype(F32)).astype(BF16)
    grouped = dot(high, gather) + dot(low, gather)
    for side in range(2):
        total = None
        for block in range(16):
            first = (16 * side + block) * 24
            strip = grouped[first : first + 24]
            strip = pltpu.roll(strip, 8 * block, 1) if block else strip
            total = strip if total is None else total + strip
        for place in range(side, TEAM, 2):
            r.sum_mine[place, 8:11] = total[3 * (place // 2) : 3 * (place // 2) + 3]


def backward_chunk(r, chunk):
    for side, lanes in enumerate(halves()):
        totals = [[], [], []]
        for part in range(3):
            r.grads[chunk, part, side, COUNT:] = r.grad_halo[chunk, part, :, lanes].astype(F32)
        for strip in strips(32):
            masks = [r.back_short[lag, strip] for lag in range(6)]
            for part in range(3):
                window = lambda lag: r.grads[chunk, part, side, strip.start + lag : strip.stop + lag]
                totals[part].append(filter_strip(r, chunk, part, lanes, window, masks))
        rows = pl.ds(pl.multiple_of(chunk * WIDE + LANES * side, LANES), LANES)
        for part in range(3):
            r.out[part, rows] = jnp.transpose(jnp.concatenate(totals[part], axis=0)).astype(BF16)


OPERANDS = ["lengths", "raw_hbm", "short", "medium", "span", "cot_hbm"]
RESULTS = ["out", "short_out", "medium_out"]


def scratch(cap, chunks, groups):
    vmem = pltpu.VMEM
    dma = pltpu.SemaphoreType.DMA
    return {
        "raw": vmem((chunks, 3, cap, WIDE), BF16),
        "cot": vmem((chunks, WIDE, COUNT), BF16),
        "tail_out": vmem((chunks, TAIL_ROWS // 16, 16, WIDE), BF16),
        "edges": vmem((chunks, 8, 16, WIDE), BF16),
        "own_pick": vmem((LEAD + COUNT, cap), BF16),
        "edge_pick": vmem((3, LEAD + COUNT, LANES), BF16),
        "tail_pick": vmem((3, TAIL_ROWS, cap), BF16),
        "fore_short": vmem((6, COUNT, LANES), F32),
        "back_short": vmem((6, COUNT, LANES), F32),
        "taps": vmem((chunks, 3, 8, WIDE), F32),
        "rows": vmem((chunks, 3, 2, LEAD + COUNT, LANES), F32),
        "filtered": vmem((chunks, 2, COUNT, WIDE), F32),
        "cot_rows": vmem((chunks, COUNT, WIDE), F32),
        "mixed": vmem((chunks, HALF + COUNT, WIDE), BF16),
        "weighted": vmem((chunks, COUNT + HALF, WIDE), BF16),
        "fore_rows": vmem((groups, LANES), F32),
        "back_rows": vmem((groups, LANES), F32),
        "fore_mask": vmem((2, HALF, LANES), BF16),
        "back_mask": vmem((2, HALF, LANES), BF16),
        "back_mask32": vmem((2, HALF, LANES), F32),
        "grads": vmem((chunks, 3, 2, COUNT + 16, LANES), F32),
        "grad_head": vmem((chunks, 3, HEAD_ROWS, WIDE), BF16),
        "grad_halo": vmem((chunks, 3, HEAD_ROWS, WIDE), BF16),
        "corr": vmem((groups, 8, LANES), F32),
        "short_parts": vmem((chunks * 2 * 24, 8, LANES), F32),
        "live_out": vmem((2, 8, LANES), I32),
        "live_near": vmem((INNER, 8, LANES), I32),
        "live_far": vmem((INNER, 8, LANES), I32),
        "sum_mine": vmem((TEAM, 11, LANES), F32),
        "sum_first": vmem((TEAM, 11, LANES), F32),
        "sum_second": vmem((TEAM, 11, LANES), F32),
        "sum_all": vmem((TEAM, 11, LANES), F32),
        "short_all": vmem((24, groups), F32),
        "load_sem": dma((2, chunks)),
        "send_sem": dma((5,)),
        "recv_sem": dma((5, chunks)),
        "live_send": dma((2,)),
        "live_recv": dma((2,)),
        "sum_send": dma((3,)),
        "sum_recv": dma((3,)),
    }


def kernel(names, scale, *refs):
    r = types.SimpleNamespace(**dict(zip(names, refs)))
    r.cap = r.raw.shape[2]
    chunks = r.raw.shape[0]
    x, me = lax.axis_index("dp"), lax.axis_index("ctx")
    dp_count, ctx_count = lax.axis_size("dp"), lax.axis_size("ctx")
    right, left = lax.rem(me + 1, ctx_count), lax.rem(me + ctx_count - 1, ctx_count)
    row, col = lax.div(me, INNER), lax.rem(me, INNER)
    y, core = lax.div(col, 2), lax.rem(col, 2)
    place1, place2 = row * 2 + core, x * 4 + y

    def near_peer(hop):
        return {"ctx": row * INNER + lax.rem(col + hop, INNER)}

    def far_peer(hop):
        return {"ctx": lax.rem(row + hop, INNER) * INNER + col}

    def peer1(other):
        return {"dp": x, "ctx": lax.div(other, 2) * INNER + y * 2 + lax.rem(other, 2)}

    def peer2(other):
        return {"dp": lax.div(other, 4), "ctx": row * INNER + lax.rem(other, 4) * 2 + core}

    def remote(src, dst, send, recv, device):
        return pltpu.make_async_remote_copy(
            src, dst, send, recv, device_id=device, device_id_type=MESH
        )

    def load_raw(c):
        lanes = pl.ds(pl.multiple_of(c * WIDE, WIDE), WIDE)
        return pltpu.make_async_copy(r.raw_hbm.at[:, :, lanes], r.raw.at[c], r.load_sem.at[0, c])

    def load_cot(c):
        rows = pl.ds(pl.multiple_of(c * WIDE, WIDE), WIDE)
        return pltpu.make_async_copy(r.cot_hbm.at[rows], r.cot.at[c], r.load_sem.at[1, c])

    def send_tail(c):
        dst = r.edges.at[c, 0 : TAIL_ROWS // 16]
        return remote(r.tail_out.at[c], dst, r.send_sem.at[0], r.recv_sem.at[0, c], {"ctx": right})

    def send_head(c):
        src, dst = r.raw.at[c, :, 0:HEAD_ROWS], r.edges.at[c, TAIL_ROWS // 16 : 8]
        return remote(src, dst, r.send_sem.at[1], r.recv_sem.at[1, c], {"ctx": left})

    def send_mixed(c):
        src, dst = r.mixed.at[c, COUNT : COUNT + HALF], r.mixed.at[c, 0:HALF]
        return remote(src, dst, r.send_sem.at[2], r.recv_sem.at[2, c], {"ctx": right})

    def send_weighted(c):
        src, dst = r.weighted.at[c, 0:HALF], r.weighted.at[c, COUNT : COUNT + HALF]
        return remote(src, dst, r.send_sem.at[3], r.recv_sem.at[3, c], {"ctx": left})

    def send_grad(c):
        src, dst = r.grad_head.at[c], r.grad_halo.at[c]
        return remote(src, dst, r.send_sem.at[4], r.recv_sem.at[4, c], {"ctx": left})

    def live_copies(stage):
        near = stage == 0
        inbox = r.live_near if near else r.live_far
        return [
            remote(
                r.live_out.at[stage],
                inbox.at[INNER - hop],
                r.live_send.at[stage],
                r.live_recv.at[stage],
                near_peer(hop) if near else far_peer(hop),
            )
            for hop in range(1, INNER)
        ]

    def sum_copies(stage, source, target, peer, place):
        copies = []
        for hop in range(1, TEAM):
            other = lax.rem(place + hop, TEAM)
            copies.append(
                remote(
                    source(other),
                    target(TEAM - hop),
                    r.sum_send.at[stage],
                    r.sum_recv.at[stage],
                    peer(other),
                )
            )
        return copies

    def start(copies):
        for copy in copies:
            copy.start()

    def take(ref, sem):
        pltpu.make_async_copy(ref, ref, sem).wait()

    def finish_live(stage):
        some = r.live_near.at[1:INNER]
        take(some, r.live_send.at[stage])
        take(some, r.live_recv.at[stage])

    def finish_sum(stage):
        some = r.sum_first.at[1:TEAM]
        take(some, r.sum_send.at[stage])
        take(some, r.sum_recv.at[stage])

    def each(step, first=0, last=chunks):
        def body(c, carry):
            step(c)
            return carry

        lax.fori_loop(first, last, body, 0)

    barrier = pltpu.get_barrier_semaphore()
    peers = [{"ctx": right}, {"ctx": left}]
    peers += [near_peer(hop) for hop in range(1, INNER)]
    peers += [far_peer(hop) for hop in range(1, INNER)]
    peers += [{"dp": lax.rem(x + hop, dp_count)} for hop in range(1, dp_count)]

    def loads(c):
        load_raw(c).start()

    each(loads)
    for peer in peers:
        pl.semaphore_signal(barrier, inc=1, device_id=peer, device_id_type=MESH)

    def cot_loads(c):
        load_cot(c).start()

    each(cot_loads)
    live = r.lengths[0, 0] + r.lengths[0, 1]
    r.live_out[0] = jnp.zeros((8, LANES), I32) + live
    build_tables(r)

    def tails(c):
        load_raw(c).wait()
        tail_chunk(r, c)

    each(tails, 0, chunks // 2)
    pl.semaphore_wait(barrier, len(peers))
    start(live_copies(0))

    def edges(c):
        send_tail(c).start()
        send_head(c).start()

    each(edges, 0, chunks // 2)
    finish_live(0)
    ahead = jnp.zeros((8, LANES), I32)
    whole = r.live_out[0]
    for hop in range(1, INNER):
        value = r.live_near[hop]
        whole = whole + value
        ahead = ahead + value * jnp.where(col + hop >= INNER, 1, 0)
    r.live_out[1] = whole
    start(live_copies(1))

    def tails_edges(c):
        tails(c)
        edges(c)

    each(tails_edges, chunks // 2, chunks)

    def widen(c):
        widen_taps(r, c)
        load_cot(c).wait()

    each(widen)
    finish_live(1)
    for hop in range(1, INNER):
        ahead = ahead + r.live_far[hop] * jnp.where(row + hop >= INNER, 1, 0)
    build_picks(r, ahead[0:1, 0:1] - me * COUNT)

    def forward(c):
        send_tail(c).wait_recv()
        send_head(c).wait_recv()
        forward_chunk(r, c)
        send_mixed(c).start()
        send_weighted(c).start()

    each(forward)

    def medium(c):
        send_mixed(c).wait_recv()
        send_weighted(c).wait_recv()
        medium_chunk(r, c)
        send_grad(c).start()
        short_sums_chunk(r, c)

    each(medium)
    medium_sums(r)
    short_sums(r)
    spread_out = sum_copies(
        0, lambda o: r.sum_mine.at[o], lambda h: r.sum_first.at[h], peer1, place1
    )
    start(spread_out)

    def backward(c):
        send_grad(c).wait_recv()
        backward_chunk(r, c)

    each(backward, 0, chunks * 3 // 8)
    finish_sum(0)
    total = r.sum_mine[place1]
    for hop in range(1, TEAM):
        total = total + r.sum_first[hop]
    r.sum_second[0] = total
    across = sum_copies(
        1, lambda o: r.sum_second.at[0], lambda h: r.sum_second.at[h], peer2, place2
    )
    start(across)
    each(backward, chunks * 3 // 8, chunks * 3 // 4)
    finish_sum(1)
    total = jnp.zeros((11, LANES), F32)
    for other in range(TEAM):
        total = total + r.sum_second[lax.rem(other - place2 + TEAM, TEAM)]
    r.sum_all[place1] = total * (1.0 / scale)
    handed = sum_copies(
        2, lambda o: r.sum_all.at[place1], lambda h: r.sum_all.at[place1], peer1, place1
    )
    start(handed)
    each(backward, chunks * 3 // 4, chunks)
    finish_sum(2)
    for place in range(TEAM):
        strip, side = place // 2, place % 2
        lanes = slice(LANES * side, LANES * side + LANES)
        r.medium_out[8 * strip : 8 * strip + 8, lanes] = r.sum_all[place, 0:8]
        r.short_all[3 * strip : 3 * strip + 3, lanes] = r.sum_all[place, 8:11]
    for part in range(3):
        r.short_out[part] = r.short_all[7 * part : 7 * part + 7]

    take(r.tail_out, r.send_sem.at[0])
    take(r.grad_head, r.send_sem.at[1])
    take(r.mixed.at[:, 0:HALF], r.send_sem.at[2])
    take(r.weighted.at[:, 0:HALF], r.send_sem.at[3])
    take(r.grad_head, r.send_sem.at[4])


def shards(raw_qkv, block_lengths, short_filter, medium_filter, doc_span, cotangent):
    count = cotangent.shape[2]
    width = cotangent.shape[1]
    groups = medium_filter.shape[0]
    group_size = width // groups
    raw = jnp.transpose(raw_qkv[0], (0, 2, 1))
    short = jnp.transpose(short_filter, (0, 2, 1))
    filt = jnp.transpose(medium_filter)
    scale = math.sqrt(lax.axis_size("dp") * lax.axis_size("ctx") * count * group_size)
    space = scratch(raw.shape[1], width // WIDE, groups)
    vmem = pl.BlockSpec(memory_space=pltpu.VMEM)
    anywhere = pl.BlockSpec(memory_space=pl.ANY)
    out, short_sum, medium_sum = pl.pallas_call(
        functools.partial(kernel, OPERANDS + RESULTS + list(space), scale),
        in_specs=[pl.BlockSpec(memory_space=pltpu.SMEM), anywhere, vmem, vmem, vmem, anywhere],
        out_specs=[vmem, vmem, vmem],
        out_shape=[
            pltpu.VMEM((3, width, count), BF16),
            jax.ShapeDtypeStruct((3, 7, groups), F32),
            jax.ShapeDtypeStruct((64, groups), F32),
        ],
        scratch_shapes=list(space.values()),
        compiler_params=pltpu.CompilerParams(
            collective_id=0, has_side_effects=True, vmem_limit_bytes=56 * 1024 * 1024
        ),
    )(block_lengths[0], raw, short, filt, doc_span[0], cotangent[0])
    return (out[None], jnp.transpose(short_sum, (0, 2, 1)), jnp.transpose(medium_sum))


def solution(mesh):
    return jax.shard_map(
        shards,
        mesh=mesh,
        in_specs=(
            P("dp", None, None, "ctx"),
            P("dp", "ctx", None),
            P(),
            P(),
            P("dp", None, "ctx"),
            P("dp", None, "ctx"),
        ),
        out_specs=(P("dp", None, None, "ctx"), P(), P()),
        check_vma=False,
    )
```

```python
import functools
import math
import types

import jax
import jax.numpy as jnp
from jax import lax
from jax.experimental import pallas as pl
from jax.experimental.pallas import tpu as pltpu
from jax.sharding import PartitionSpec as P

F32 = jnp.float32
BF16 = jnp.bfloat16
I32 = jnp.int32
MESH = pl.DeviceIdType.MESH
LANES = 128
WIDE = 256
REACH = 22
TAIL_ROWS = 80
HEAD_ROWS = 16
LEAD = 8
HALF = 64
COUNT = 128
TEAM = 16
INNER = 8


def iota(shape, dim):
    return lax.broadcasted_iota(I32, shape, dim)


def ones_where(condition, dtype=BF16):
    return jnp.where(condition, 1.0, 0.0).astype(dtype)


def dot(left, right):
    return jnp.dot(left, right, preferred_element_type=F32)


def dot_columns(left, right):
    return lax.dot_general(left, right, (((0,), (0,)), ((), ())), preferred_element_type=F32)


def column_of(row):
    return jnp.transpose(jnp.broadcast_to(row, (LANES, LANES)))


def halves():
    return [slice(LANES * side, LANES * side + LANES) for side in range(WIDE // LANES)]


def build_tables(r):
    before, after = column_of(r.span[0:1]), column_of(r.span[1:2])
    for lag in range(1, 7):
        r.fore_short[lag - 1] = ones_where(before >= lag, F32)
        r.back_short[lag - 1] = ones_where(after >= lag, F32)
    taps = r.medium.shape[0]
    source = iota((taps, LANES), 0)
    lane = iota((taps, LANES), 1)
    filt = r.medium[...].astype(BF16)
    r.fore_rows[...] = dot_columns(filt, ones_where(lane == taps - source))
    r.back_rows[...] = dot_columns(filt, ones_where(lane == source))
    row = iota((HALF, LANES), 0)
    lane = iota((HALF, LANES), 1)
    for half in range(2):
        part = slice(HALF * half, HALF * half + HALF)
        lag = row + HALF - lane
        r.fore_mask[half] = ones_where((lag >= 0) & (lag < taps) & (lag <= before[part]))
        lag = lane - row
        back = (lag >= 0) & (lag < taps) & (lag <= after[part])
        r.back_mask[half] = ones_where(back)
        r.back_mask32[half] = ones_where(back, F32)
    live = r.lengths[0, 0] + r.lengths[0, 1]
    place = iota((TAIL_ROWS, r.cap), 0)
    column = iota((TAIL_ROWS, r.cap), 1)
    for part in range(3):
        step = place - REACH * part
        pick = (step >= 0) & (step < REACH) & (column == live - REACH + step)
        r.tail_pick[part] = ones_where(pick)


def widen_taps(r, chunk):
    span = LANES * 16 // WIDE
    owner = lax.rem(chunk, span) * (WIDE // 16) + iota((LANES, WIDE), 1) // 16
    spread = ones_where(iota((LANES, WIDE), 0) == owner)
    window = pl.ds(pl.multiple_of(lax.div(chunk, span) * LANES, LANES), LANES)
    for part in range(3):
        r.taps[chunk, part, 0:7] = dot(r.short[part, :, window].astype(BF16), spread)


def tail_chunk(r, chunk):
    total = dot(r.tail_pick[0], r.raw[chunk, 0])
    for part in range(1, 3):
        total = total + dot(r.tail_pick[part], r.raw[chunk, part])
    r.tail_out[chunk] = total.astype(BF16).reshape(TAIL_ROWS // 16, 16, WIDE)


def build_picks(r, drift):
    live = r.lengths[0, 0] + r.lengths[0, 1]
    shape = (LEAD + COUNT, r.cap)
    token = iota(shape, 0) - LEAD - jnp.broadcast_to(drift, shape)
    column = iota(shape, 1)
    r.own_pick[...] = ones_where((column == token) & (column < live))
    shape = (LEAD + COUNT, LANES)
    token = iota(shape, 0) - LEAD - jnp.broadcast_to(drift, shape)
    column = iota(shape, 1)
    for part in range(3):
        late = token + REACH
        from_tail = (late >= 0) & (late < REACH) & (column == REACH * part + late)
        over = token - live
        from_head = (over >= 0) & (column == TAIL_ROWS + HEAD_ROWS * part + over)
        r.edge_pick[part] = ones_where(from_tail | from_head)


def strips(rows):
    return [slice(first, first + rows) for first in range(0, COUNT, rows)]


def filter_strip(r, chunk, part, lanes, window, masks):
    total = r.taps[chunk, part, 0:1, lanes] * window(0)
    for lag in range(1, 7):
        total = total + r.taps[chunk, part, lag : lag + 1, lanes] * (masks[lag - 1] * window(lag))
    return total


def turn_chunk(r, chunk):
    for lanes in halves():
        r.cot_rows[chunk, :, lanes] = jnp.transpose(r.cot[chunk, lanes].astype(F32))


def forward_chunk(r, chunk):
    edges = r.edges[chunk].reshape(COUNT, WIDE)
    for part in range(3):
        packed = dot(r.own_pick[...], r.raw[chunk, part]) + dot(r.edge_pick[part], edges)
        for side, lanes in enumerate(halves()):
            r.rows[chunk, part, side] = packed[:, lanes]
    for side, lanes in enumerate(halves()):
        for strip in strips(32):
            masks = [r.fore_short[lag, strip] for lag in range(6)]
            query, key, value = [
                filter_strip(
                    r,
                    chunk,
                    part,
                    lanes,
                    lambda lag: r.rows[chunk, part, side, LEAD + strip.start - lag : LEAD + strip.stop - lag],
                    masks,
                )
                for part in range(3)
            ]
            r.filtered[chunk, 0, strip, lanes] = key
            r.filtered[chunk, 1, strip, lanes] = value
            r.mixed[chunk, HALF + strip.start : HALF + strip.stop, lanes] = (key * value).astype(BF16)
            r.weighted[chunk, strip, lanes] = (r.cot_rows[chunk, strip, lanes] * query).astype(BF16)


def toeplitz(rows, g):
    row = jnp.broadcast_to(rows[g : g + 1], (HALF, LANES)).astype(BF16)
    return pltpu.roll(row, 0, 1, stride=1, stride_axis=0)


def own_lanes(every, pair_of):
    result = every[:HALF]
    for pair in range(1, 4):
        result = jnp.where(pair_of == pair, every[HALF * pair : HALF * pair + HALF], result)
    return result


def paired(bands, mask):
    bands = [band * mask for band in bands]
    pairs = [jnp.concatenate(bands[2 * p : 2 * p + 2], axis=1) for p in range(4)]
    return jnp.concatenate(pairs, axis=0)


def bands_chunk(r, chunk):
    for side in range(2):
        first = pl.multiple_of(chunk * 16 + 8 * side, 8)
        fore = r.fore_rows[pl.ds(first, 8)]
        back = r.back_rows[pl.ds(first, 8)]
        fores = [toeplitz(fore, g) for g in range(8)]
        backs = [toeplitz(back, g) for g in range(8)]
        for half in range(2):
            r.fore_bands[chunk, side, half] = paired(fores, r.fore_mask[half])
            r.back_bands[chunk, side, half] = paired(backs, r.back_mask[half])


def medium_chunk(r, chunk):
    shape = (HALF + COUNT, LANES)
    even = iota(shape, 1) // 16 % 2 == 0
    pair_of = iota((HALF, LANES), 1) // 32
    for side, lanes in enumerate(halves()):
        first = pl.multiple_of(chunk * 16 + 8 * side, 8)
        mixed = r.mixed[chunk, :, lanes]
        weighted = r.weighted[chunk, :, lanes]
        zero = jnp.zeros(shape, BF16)
        mixed_of = [jnp.where(even, mixed, zero), jnp.where(even, zero, mixed)]
        weighted_of = [jnp.where(even, weighted, zero), jnp.where(even, zero, weighted)]
        corr = [None] * 8
        for half in range(2):
            part = slice(HALF * half, HALF * half + HALF)
            window = slice(HALF * half, HALF * half + 2 * HALF)
            earlier = jnp.concatenate([m[window] for m in mixed_of], axis=0)
            later = jnp.concatenate([w[window] for w in weighted_of], axis=0)
            response = own_lanes(dot(r.fore_bands[chunk, side, half], earlier), pair_of)
            spread = own_lanes(dot(r.back_bands[chunk, side, half], later), pair_of)
            grads = (
                r.cot_rows[chunk, part, lanes] * response,
                spread * r.filtered[chunk, 1, part, lanes],
                spread * r.filtered[chunk, 0, part, lanes],
            )
            for b in range(3):
                grad = grads[b].astype(BF16)
                if half == 0:
                    r.grad_head[chunk, b, :, lanes] = grad[:HEAD_ROWS]
                r.grads[chunk, b, side, part] = grad.astype(F32)
            own = mixed[HALF + HALF * half : 2 * HALF + HALF * half]
            alone = [jnp.where(pair_of == p, own, zero[:HALF]) for p in range(4)]
            turned = jnp.transpose(weighted[window])
            blank = jnp.zeros((16, LANES), BF16)
            sides = []
            for parity in range(2):
                blocks = [turned[16 * g : 16 * g + 16] if g % 2 == parity else blank for g in range(8)]
                sides.append(jnp.concatenate(blocks, axis=0))
            every = dot(jnp.concatenate(alone, axis=0), jnp.concatenate(sides, axis=1))
            mask = r.back_mask32[half]
            for g in range(8):
                tile = every[HALF * (g // 2) : HALF * (g // 2) + HALF]
                term = tile[:, LANES * (g % 2) : LANES * (g % 2) + LANES] * mask
                corr[g] = term if half == 0 else corr[g] + term
        for g in range(8):
            total = corr[g][0:8]
            for strip in range(1, 8):
                total = total + pltpu.roll(corr[g][8 * strip : 8 * strip + 8], LANES - 8 * strip, 1)
            r.corr[first + g] = total


def medium_sums(r):
    total = None
    for row in range(8):
        strip = r.corr[:, row, :]
        strip = strip if row == 0 else pltpu.roll(strip, LANES - row, 1)
        total = strip if total is None else total + strip
    total = jnp.transpose(total)
    for place in range(TEAM):
        strip, side = place // 2, place % 2
        r.sum_mine[place, 0:8] = total[8 * strip : 8 * strip + 8, LANES * side : LANES * side + LANES]


def short_sums_chunk(r, chunk):
    for side, lanes in enumerate(halves()):
        sums = [None] * 24
        for strip in strips(16):
            masks = [r.fore_short[lag, strip] for lag in range(6)]
            for part in range(3):
                grad = r.grads[chunk, part, side, strip]
                for lag in range(7):
                    window = r.rows[chunk, part, side, LEAD + strip.start - lag : LEAD + strip.stop - lag]
                    term = grad * window if lag == 0 else (masks[lag - 1] * grad) * window
                    term = term[0:8] + term[8:16]
                    place = 7 * part + lag
                    sums[place] = term if sums[place] is None else sums[place] + term
        for place in range(21):
            r.short_parts[(chunk * 2 + side) * 24 + place] = sums[place]


def short_sums(r):
    total = jnp.sum(r.short_parts[...], axis=1)
    gather = ones_where(iota((LANES, LANES), 1) == iota((LANES, LANES), 0) // 16)
    high = total.astype(BF16)
    low = (total - high.astype(F32)).astype(BF16)
    grouped = dot(high, gather) + dot(low, gather)
    for side in range(2):
        total = None
        for block in range(16):
            first = (16 * side + block) * 24
            strip = grouped[first : first + 24]
            strip = pltpu.roll(strip, 8 * block, 1) if block else strip
            total = strip if total is None else total + strip
        for place in range(side, TEAM, 2):
            r.sum_mine[place, 8:11] = total[3 * (place // 2) : 3 * (place // 2) + 3]


def backward_chunk(r, chunk):
    for side, lanes in enumerate(halves()):
        totals = [[], [], []]
        for part in range(3):
            r.grads[chunk, part, side, COUNT:] = r.grad_halo[chunk, part, :, lanes].astype(F32)
        for strip in strips(32):
            masks = [r.back_short[lag, strip] for lag in range(6)]
            for part in range(3):
                window = lambda lag: r.grads[chunk, part, side, strip.start + lag : strip.stop + lag]
                totals[part].append(filter_strip(r, chunk, part, lanes, window, masks))
        rows = pl.ds(pl.multiple_of(chunk * WIDE + LANES * side, LANES), LANES)
        for part in range(3):
            r.out[part, rows] = jnp.transpose(jnp.concatenate(totals[part], axis=0)).astype(BF16)


OPERANDS = ["lengths", "raw_hbm", "short", "medium", "span", "cot_hbm"]
RESULTS = ["out", "short_out", "medium_out"]


def scratch(cap, chunks, groups):
    vmem = pltpu.VMEM
    dma = pltpu.SemaphoreType.DMA
    return {
        "raw": vmem((chunks, 3, cap, WIDE), BF16),
        "cot": vmem((chunks, WIDE, COUNT), BF16),
        "tail_out": vmem((chunks, TAIL_ROWS // 16, 16, WIDE), BF16),
        "edges": vmem((chunks, 8, 16, WIDE), BF16),
        "own_pick": vmem((LEAD + COUNT, cap), BF16),
        "edge_pick": vmem((3, LEAD + COUNT, LANES), BF16),
        "tail_pick": vmem((3, TAIL_ROWS, cap), BF16),
        "fore_short": vmem((6, COUNT, LANES), F32),
        "back_short": vmem((6, COUNT, LANES), F32),
        "taps": vmem((chunks, 3, 8, WIDE), F32),
        "rows": vmem((chunks, 3, 2, LEAD + COUNT, LANES), F32),
        "filtered": vmem((chunks, 2, COUNT, WIDE), F32),
        "cot_rows": vmem((chunks, COUNT, WIDE), F32),
        "mixed": vmem((chunks, HALF + COUNT, WIDE), BF16),
        "weighted": vmem((chunks, COUNT + HALF, WIDE), BF16),
        "fore_rows": vmem((groups, LANES), F32),
        "back_rows": vmem((groups, LANES), F32),
        "fore_mask": vmem((2, HALF, LANES), BF16),
        "back_mask": vmem((2, HALF, LANES), BF16),
        "back_mask32": vmem((2, HALF, LANES), F32),
        "grads": vmem((chunks, 3, 2, COUNT + 16, LANES), F32),
        "grad_head": vmem((chunks, 3, HEAD_ROWS, WIDE), BF16),
        "grad_halo": vmem((chunks, 3, HEAD_ROWS, WIDE), BF16),
        "fore_bands": vmem((chunks, 2, 2, 4 * HALF, 4 * HALF), BF16),
        "back_bands": vmem((chunks, 2, 2, 4 * HALF, 4 * HALF), BF16),
        "corr": vmem((groups, 8, LANES), F32),
        "short_parts": vmem((chunks * 2 * 24, 8, LANES), F32),
        "live_out": vmem((2, 8, LANES), I32),
        "live_near": vmem((INNER, 8, LANES), I32),
        "live_far": vmem((INNER, 8, LANES), I32),
        "sum_mine": vmem((TEAM, 11, LANES), F32),
        "sum_first": vmem((TEAM, 11, LANES), F32),
        "sum_second": vmem((TEAM, 11, LANES), F32),
        "sum_all": vmem((TEAM, 11, LANES), F32),
        "short_all": vmem((24, groups), F32),
        "load_sem": dma((2, chunks)),
        "send_sem": dma((5,)),
        "recv_sem": dma((5, chunks)),
        "live_send": dma((2,)),
        "live_recv": dma((2,)),
        "sum_send": dma((3,)),
        "sum_recv": dma((3,)),
    }


def kernel(names, scale, *refs):
    r = types.SimpleNamespace(**dict(zip(names, refs)))
    r.cap = r.raw.shape[2]
    chunks = r.raw.shape[0]
    x, me = lax.axis_index("dp"), lax.axis_index("ctx")
    dp_count, ctx_count = lax.axis_size("dp"), lax.axis_size("ctx")
    right, left = lax.rem(me + 1, ctx_count), lax.rem(me + ctx_count - 1, ctx_count)
    row, col = lax.div(me, INNER), lax.rem(me, INNER)
    y, core = lax.div(col, 2), lax.rem(col, 2)
    place1, place2 = row * 2 + core, x * 4 + y

    def near_peer(hop):
        return {"ctx": row * INNER + lax.rem(col + hop, INNER)}

    def far_peer(hop):
        return {"ctx": lax.rem(row + hop, INNER) * INNER + col}

    def peer1(other):
        return {"dp": x, "ctx": lax.div(other, 2) * INNER + y * 2 + lax.rem(other, 2)}

    def peer2(other):
        return {"dp": lax.div(other, 4), "ctx": row * INNER + lax.rem(other, 4) * 2 + core}

    def remote(src, dst, send, recv, device):
        return pltpu.make_async_remote_copy(
            src, dst, send, recv, device_id=device, device_id_type=MESH
        )

    def load_raw(c):
        lanes = pl.ds(pl.multiple_of(c * WIDE, WIDE), WIDE)
        return pltpu.make_async_copy(r.raw_hbm.at[:, :, lanes], r.raw.at[c], r.load_sem.at[0, c])

    def load_cot(c):
        rows = pl.ds(pl.multiple_of(c * WIDE, WIDE), WIDE)
        return pltpu.make_async_copy(r.cot_hbm.at[rows], r.cot.at[c], r.load_sem.at[1, c])

    def send_tail(c):
        dst = r.edges.at[c, 0 : TAIL_ROWS // 16]
        return remote(r.tail_out.at[c], dst, r.send_sem.at[0], r.recv_sem.at[0, c], {"ctx": right})

    def send_head(c):
        src, dst = r.raw.at[c, :, 0:HEAD_ROWS], r.edges.at[c, TAIL_ROWS // 16 : 8]
        return remote(src, dst, r.send_sem.at[1], r.recv_sem.at[1, c], {"ctx": left})

    def send_mixed(c):
        src, dst = r.mixed.at[c, COUNT : COUNT + HALF], r.mixed.at[c, 0:HALF]
        return remote(src, dst, r.send_sem.at[2], r.recv_sem.at[2, c], {"ctx": right})

    def send_weighted(c):
        src, dst = r.weighted.at[c, 0:HALF], r.weighted.at[c, COUNT : COUNT + HALF]
        return remote(src, dst, r.send_sem.at[3], r.recv_sem.at[3, c], {"ctx": left})

    def send_grad(c):
        src, dst = r.grad_head.at[c], r.grad_halo.at[c]
        return remote(src, dst, r.send_sem.at[4], r.recv_sem.at[4, c], {"ctx": left})

    def live_copies(stage):
        near = stage == 0
        inbox = r.live_near if near else r.live_far
        return [
            remote(
                r.live_out.at[stage],
                inbox.at[INNER - hop],
                r.live_send.at[stage],
                r.live_recv.at[stage],
                near_peer(hop) if near else far_peer(hop),
            )
            for hop in range(1, INNER)
        ]

    def sum_copies(stage, source, target, peer, place):
        copies = []
        for hop in range(1, TEAM):
            other = lax.rem(place + hop, TEAM)
            copies.append(
                remote(
                    source(other),
                    target(TEAM - hop),
                    r.sum_send.at[stage],
                    r.sum_recv.at[stage],
                    peer(other),
                )
            )
        return copies

    def start(copies):
        for copy in copies:
            copy.start()

    def take(ref, sem):
        pltpu.make_async_copy(ref, ref, sem).wait()

    def finish_live(stage):
        some = r.live_near.at[1:INNER]
        take(some, r.live_send.at[stage])
        take(some, r.live_recv.at[stage])

    def finish_sum(stage):
        some = r.sum_first.at[1:TEAM]
        take(some, r.sum_send.at[stage])
        take(some, r.sum_recv.at[stage])

    def each(step, first=0, last=chunks):
        def body(c, carry):
            step(c)
            return carry

        lax.fori_loop(first, last, body, 0)

    barrier = pltpu.get_barrier_semaphore()
    peers = [{"ctx": right}, {"ctx": left}]
    peers += [near_peer(hop) for hop in range(1, INNER)]
    peers += [far_peer(hop) for hop in range(1, INNER)]
    peers += [{"dp": lax.rem(x + hop, dp_count)} for hop in range(1, dp_count)]

    def loads(c):
        load_raw(c).start()

    each(loads)
    for peer in peers:
        pl.semaphore_signal(barrier, inc=1, device_id=peer, device_id_type=MESH)

    def cot_loads(c):
        load_cot(c).start()

    each(cot_loads)
    live = r.lengths[0, 0] + r.lengths[0, 1]
    r.live_out[0] = jnp.zeros((8, LANES), I32) + live
    build_tables(r)

    def tails(c):
        load_raw(c).wait()
        tail_chunk(r, c)

    def widen(c):
        widen_taps(r, c)

    each(tails)
    each(widen)
    pl.semaphore_wait(barrier, len(peers))
    start(live_copies(0))

    def edges(c):
        send_tail(c).start()
        send_head(c).start()

    each(edges)

    def bands(c):
        load_cot(c).wait()
        turn_chunk(r, c)
        bands_chunk(r, c)

    each(bands, 0, chunks // 2)
    finish_live(0)
    ahead = jnp.zeros((8, LANES), I32)
    whole = r.live_out[0]
    for hop in range(1, INNER):
        value = r.live_near[hop]
        whole = whole + value
        ahead = ahead + value * jnp.where(col + hop >= INNER, 1, 0)
    r.live_out[1] = whole
    start(live_copies(1))

    each(bands, chunks // 2, chunks)
    finish_live(1)
    for hop in range(1, INNER):
        ahead = ahead + r.live_far[hop] * jnp.where(row + hop >= INNER, 1, 0)
    build_picks(r, ahead[0:1, 0:1] - me * COUNT)

    def forward(c):
        send_tail(c).wait_recv()
        send_head(c).wait_recv()
        forward_chunk(r, c)
        send_mixed(c).start()
        send_weighted(c).start()

    each(forward)

    def medium(c):
        send_mixed(c).wait_recv()
        send_weighted(c).wait_recv()
        medium_chunk(r, c)
        send_grad(c).start()
        short_sums_chunk(r, c)

    each(medium)
    medium_sums(r)
    short_sums(r)
    spread_out = sum_copies(
        0, lambda o: r.sum_mine.at[o], lambda h: r.sum_first.at[h], peer1, place1
    )
    start(spread_out)

    def backward(c):
        send_grad(c).wait_recv()
        backward_chunk(r, c)

    each(backward, 0, chunks * 3 // 8)
    finish_sum(0)
    total = r.sum_mine[place1]
    for hop in range(1, TEAM):
        total = total + r.sum_first[hop]
    r.sum_second[0] = total
    across = sum_copies(
        1, lambda o: r.sum_second.at[0], lambda h: r.sum_second.at[h], peer2, place2
    )
    start(across)
    each(backward, chunks * 3 // 8, chunks * 3 // 4)
    finish_sum(1)
    total = jnp.zeros((11, LANES), F32)
    for other in range(TEAM):
        total = total + r.sum_second[lax.rem(other - place2 + TEAM, TEAM)]
    r.sum_all[place1] = total * (1.0 / scale)
    handed = sum_copies(
        2, lambda o: r.sum_all.at[place1], lambda h: r.sum_all.at[place1], peer1, place1
    )
    start(handed)
    each(backward, chunks * 3 // 4, chunks)
    finish_sum(2)
    for place in range(TEAM):
        strip, side = place // 2, place % 2
        lanes = slice(LANES * side, LANES * side + LANES)
        r.medium_out[8 * strip : 8 * strip + 8, lanes] = r.sum_all[place, 0:8]
        r.short_all[3 * strip : 3 * strip + 3, lanes] = r.sum_all[place, 8:11]
    for part in range(3):
        r.short_out[part] = r.short_all[7 * part : 7 * part + 7]

    take(r.tail_out, r.send_sem.at[0])
    take(r.grad_head, r.send_sem.at[1])
    take(r.mixed.at[:, 0:HALF], r.send_sem.at[2])
    take(r.weighted.at[:, 0:HALF], r.send_sem.at[3])
    take(r.grad_head, r.send_sem.at[4])


def shards(raw_qkv, block_lengths, short_filter, medium_filter, doc_span, cotangent):
    count = cotangent.shape[2]
    width = cotangent.shape[1]
    groups = medium_filter.shape[0]
    group_size = width // groups
    raw = jnp.transpose(raw_qkv[0], (0, 2, 1))
    short = jnp.transpose(short_filter, (0, 2, 1))
    filt = jnp.transpose(medium_filter)
    scale = math.sqrt(lax.axis_size("dp") * lax.axis_size("ctx") * count * group_size)
    space = scratch(raw.shape[1], width // WIDE, groups)
    vmem = pl.BlockSpec(memory_space=pltpu.VMEM)
    anywhere = pl.BlockSpec(memory_space=pl.ANY)
    out, short_sum, medium_sum = pl.pallas_call(
        functools.partial(kernel, OPERANDS + RESULTS + list(space), scale),
        in_specs=[pl.BlockSpec(memory_space=pltpu.SMEM), anywhere, vmem, vmem, vmem, anywhere],
        out_specs=[vmem, vmem, vmem],
        out_shape=[
            pltpu.VMEM((3, width, count), BF16),
            jax.ShapeDtypeStruct((3, 7, groups), F32),
            jax.ShapeDtypeStruct((64, groups), F32),
        ],
        scratch_shapes=list(space.values()),
        compiler_params=pltpu.CompilerParams(
            collective_id=0, has_side_effects=True, vmem_limit_bytes=56 * 1024 * 1024
        ),
    )(block_lengths[0], raw, short, filt, doc_span[0], cotangent[0])
    return (out[None], jnp.transpose(short_sum, (0, 2, 1)), jnp.transpose(medium_sum))


def solution(mesh):
    return jax.shard_map(
        shards,
        mesh=mesh,
        in_specs=(
            P("dp", None, None, "ctx"),
            P("dp", "ctx", None),
            P(),
            P(),
            P("dp", None, "ctx"),
            P("dp", None, "ctx"),
        ),
        out_specs=(P("dp", None, None, "ctx"), P(), P()),
        check_vma=False,
    )
```

```python
import functools
import math
import types

import jax
import jax.numpy as jnp
from jax import lax
from jax.experimental import pallas as pl
from jax.experimental.pallas import tpu as pltpu
from jax.sharding import PartitionSpec as P

F32 = jnp.float32
BF16 = jnp.bfloat16
I32 = jnp.int32
MESH = pl.DeviceIdType.MESH
LANES = 128
WIDE = 256
LATE = 64
REACH = 22
TAIL_ROWS = 80
HEAD_ROWS = 16
LEAD = 8
HALF = 64
FIRST_ROWS = 24
LAST_ROWS = 16
COUNT = 128
TEAM = 16
INNER = 8


def iota(shape, dim):
    return lax.broadcasted_iota(I32, shape, dim)


def ones_where(condition, dtype=BF16):
    return jnp.where(condition, 1.0, 0.0).astype(dtype)


def dot(left, right):
    return jnp.dot(left, right, preferred_element_type=F32)


def dot_columns(left, right):
    return lax.dot_general(left, right, (((0,), (0,)), ((), ())), preferred_element_type=F32)


def column_of(row):
    return jnp.transpose(jnp.broadcast_to(row, (LANES, LANES)))


def halves():
    return [slice(LANES * side, LANES * side + LANES) for side in range(WIDE // LANES)]


def build_tail_pick(r):
    live = r.lengths[0, 0] + r.lengths[0, 1]
    rows = r.cap - LATE
    shape = (TAIL_ROWS, 3 * rows)
    place, column = iota(shape, 0), iota(shape, 1)
    pick = None
    for part in range(3):
        step = place - REACH * part
        own = (step >= 0) & (step < REACH) & (column - rows * part == live - REACH + step - LATE)
        pick = own if pick is None else pick | own
    r.tail_pick[...] = ones_where(pick)


def build_tables(r):
    before, after = column_of(r.span[0:1]), column_of(r.span[1:2])
    for lag in range(1, 7):
        r.fore_short[lag - 1] = ones_where(before >= lag, F32)
        r.back_short[lag - 1] = ones_where(after >= lag, F32)
    taps = r.medium.shape[0]
    source = iota((taps, LANES), 0)
    lane = iota((taps, LANES), 1)
    filt = r.medium[...].astype(BF16)
    r.fore_rows[...] = dot_columns(filt, ones_where(lane == taps - source))
    r.back_rows[...] = dot_columns(filt, ones_where(lane == source))
    row = iota((HALF, LANES), 0)
    lane = iota((HALF, LANES), 1)
    for half in range(2):
        part = slice(HALF * half, HALF * half + HALF)
        lag = row + HALF - lane
        r.fore_mask[half] = ones_where((lag >= 0) & (lag < taps) & (lag <= before[part]))
        lag = lane - row
        back = (lag >= 0) & (lag < taps) & (lag <= after[part])
        r.back_mask[half] = ones_where(back)
        r.back_mask32[half] = ones_where(back, F32)


def widen_taps(r, chunk):
    span = LANES * 16 // WIDE
    owner = lax.rem(chunk, span) * (WIDE // 16) + iota((LANES, WIDE), 1) // 16
    spread = ones_where(iota((LANES, WIDE), 0) == owner)
    window = pl.ds(pl.multiple_of(lax.div(chunk, span) * LANES, LANES), LANES)
    blank = jnp.zeros((1, LANES), F32)
    taps = [row for part in range(3) for row in (r.short[part, :, window], blank)]
    wide = dot(jnp.concatenate(taps, axis=0).astype(BF16), spread)
    for part in range(3):
        r.taps[chunk, part] = wide[8 * part : 8 * part + 8]


def tail_chunk(r, chunk):
    total = dot(r.tail_pick[...], r.raw[chunk, :, LATE:].reshape(3 * (r.cap - LATE), WIDE))
    r.tail_out[chunk] = total.astype(BF16).reshape(TAIL_ROWS // 16, 16, WIDE)


def build_picks(r, drift):
    live = r.lengths[0, 0] + r.lengths[0, 1]
    shape = (LEAD + COUNT, r.cap)
    token = iota(shape, 0) - LEAD - jnp.broadcast_to(drift, shape)
    column = iota(shape, 1)
    r.own_pick[...] = ones_where((column == token) & (column < live))
    shape = (FIRST_ROWS, LANES)
    token = iota(shape, 0) - LEAD - jnp.broadcast_to(drift, shape)
    column = iota(shape, 1)
    for part in range(3):
        late = token + REACH
        from_tail = (late >= 0) & (late < REACH) & (column == REACH * part + late)
        r.edge_pick[FIRST_ROWS * part : FIRST_ROWS * part + FIRST_ROWS] = ones_where(from_tail, F32)
    shape = (LAST_ROWS, LANES)
    token = iota(shape, 0) + COUNT - LAST_ROWS - jnp.broadcast_to(drift, shape)
    column = iota(shape, 1)
    for part in range(3):
        over = token - live
        from_head = (over >= 0) & (column == TAIL_ROWS + HEAD_ROWS * part + over)
        first = 3 * FIRST_ROWS + LAST_ROWS * part
        r.edge_pick[first : first + LAST_ROWS] = ones_where(from_head, F32)


def strips(rows):
    return [slice(first, first + rows) for first in range(0, COUNT, rows)]


def filter_strip(r, chunk, part, lanes, window, masks):
    total = r.taps[chunk, part, 0:1, lanes] * window(0)
    for lag in range(1, 7):
        total = total + r.taps[chunk, part, lag : lag + 1, lanes] * (masks[lag - 1] * window(lag))
    return total


def forward_chunk(r, chunk):
    edges = dot(r.edge_pick[...].astype(BF16), r.edges[chunk].reshape(COUNT, WIDE))
    for part in range(3):
        packed = dot(r.own_pick[...], r.raw[chunk, part])
        first = packed[:FIRST_ROWS] + edges[FIRST_ROWS * part : FIRST_ROWS * part + FIRST_ROWS]
        place = 3 * FIRST_ROWS + LAST_ROWS * part
        last = packed[LEAD + COUNT - LAST_ROWS :] + edges[place : place + LAST_ROWS]
        middle = packed[FIRST_ROWS : LEAD + COUNT - LAST_ROWS]
        for side, lanes in enumerate(halves()):
            r.rows[chunk, part, side, :FIRST_ROWS] = first[:, lanes]
            r.rows[chunk, part, side, FIRST_ROWS : LEAD + COUNT - LAST_ROWS] = middle[:, lanes]
            r.rows[chunk, part, side, LEAD + COUNT - LAST_ROWS :] = last[:, lanes]
    for side, lanes in enumerate(halves()):
        cot = jnp.transpose(r.cot[chunk, lanes].astype(F32))
        r.cot_rows[chunk, :, lanes] = cot
        for strip in strips(32):
            masks = [r.fore_short[lag, strip] for lag in range(6)]
            query, key, value = [
                filter_strip(
                    r,
                    chunk,
                    part,
                    lanes,
                    lambda lag: r.rows[chunk, part, side, LEAD + strip.start - lag : LEAD + strip.stop - lag],
                    masks,
                )
                for part in range(3)
            ]
            r.filtered[chunk, 0, strip, lanes] = key
            r.filtered[chunk, 1, strip, lanes] = value
            r.mixed[chunk, HALF + strip.start : HALF + strip.stop, lanes] = (key * value).astype(BF16)
            r.weighted[chunk, strip, lanes] = (cot[strip] * query).astype(BF16)


def toeplitz(rows, g):
    row = jnp.broadcast_to(rows[g : g + 1], (HALF, LANES)).astype(BF16)
    return pltpu.roll(row, 0, 1, stride=1, stride_axis=0)


def own_lanes(every, pair_of):
    result = every[:HALF]
    for pair in range(1, 4):
        result = jnp.where(pair_of == pair, every[HALF * pair : HALF * pair + HALF], result)
    return result


def paired(bands, mask):
    bands = [band * mask for band in bands]
    pairs = [jnp.concatenate(bands[2 * p : 2 * p + 2], axis=1) for p in range(4)]
    return jnp.concatenate(pairs, axis=0)


def medium_chunk(r, chunk):
    shape = (HALF + COUNT, LANES)
    even = iota(shape, 1) // 16 % 2 == 0
    pair_of = iota((HALF, LANES), 1) // 32
    for side, lanes in enumerate(halves()):
        first = pl.multiple_of(chunk * 16 + 8 * side, 8)
        fore = r.fore_rows[pl.ds(first, 8)]
        back = r.back_rows[pl.ds(first, 8)]
        fores = [toeplitz(fore, g) for g in range(8)]
        backs = [toeplitz(back, g) for g in range(8)]
        mixed = r.mixed[chunk, :, lanes]
        weighted = r.weighted[chunk, :, lanes]
        zero = jnp.zeros(shape, BF16)
        mixed_of = [jnp.where(even, mixed, zero), jnp.where(even, zero, mixed)]
        weighted_of = [jnp.where(even, weighted, zero), jnp.where(even, zero, weighted)]
        corr = [None] * 8
        for half in range(2):
            part = slice(HALF * half, HALF * half + HALF)
            window = slice(HALF * half, HALF * half + 2 * HALF)
            earlier = jnp.concatenate([m[window] for m in mixed_of], axis=0)
            later = jnp.concatenate([w[window] for w in weighted_of], axis=0)
            response = own_lanes(dot(paired(fores, r.fore_mask[half]), earlier), pair_of)
            spread = own_lanes(dot(paired(backs, r.back_mask[half]), later), pair_of)
            grads = (
                r.cot_rows[chunk, part, lanes] * response,
                spread * r.filtered[chunk, 1, part, lanes],
                spread * r.filtered[chunk, 0, part, lanes],
            )
            for b in range(3):
                grad = grads[b].astype(BF16)
                if half == 0:
                    r.grad_head[chunk, b, :, lanes] = grad[:HEAD_ROWS]
                r.grads[chunk, b, side, part] = grad.astype(F32)
            own = mixed[HALF + HALF * half : 2 * HALF + HALF * half]
            alone = [jnp.where(pair_of == p, own, zero[:HALF]) for p in range(4)]
            turned = jnp.transpose(weighted[window])
            blank = jnp.zeros((16, LANES), BF16)
            sides = []
            for parity in range(2):
                blocks = [turned[16 * g : 16 * g + 16] if g % 2 == parity else blank for g in range(8)]
                sides.append(jnp.concatenate(blocks, axis=0))
            every = dot(jnp.concatenate(alone, axis=0), jnp.concatenate(sides, axis=1))
            mask = r.back_mask32[half]
            for g in range(8):
                tile = every[HALF * (g // 2) : HALF * (g // 2) + HALF]
                term = tile[:, LANES * (g % 2) : LANES * (g % 2) + LANES] * mask
                corr[g] = term if half == 0 else corr[g] + term
        for g in range(8):
            total = corr[g][0:8]
            for strip in range(1, 8):
                total = total + pltpu.roll(corr[g][8 * strip : 8 * strip + 8], LANES - 8 * strip, 1)
            r.corr[first + g] = total


def medium_sums(r):
    total = None
    for row in range(8):
        strip = r.corr[:, row, :]
        strip = strip if row == 0 else pltpu.roll(strip, LANES - row, 1)
        total = strip if total is None else total + strip
    total = jnp.transpose(total)
    for place in range(TEAM):
        strip, side = place // 2, place % 2
        r.sum_mine[place, 0:8] = total[8 * strip : 8 * strip + 8, LANES * side : LANES * side + LANES]


def short_sums_chunk(r, chunk):
    for side, lanes in enumerate(halves()):
        sums = [None] * 24
        for strip in strips(16):
            masks = [r.fore_short[lag, strip] for lag in range(6)]
            for part in range(3):
                grad = r.grads[chunk, part, side, strip]
                for lag in range(7):
                    window = r.rows[chunk, part, side, LEAD + strip.start - lag : LEAD + strip.stop - lag]
                    term = grad * window if lag == 0 else (masks[lag - 1] * grad) * window
                    term = term[0:8] + term[8:16]
                    place = 7 * part + lag
                    sums[place] = term if sums[place] is None else sums[place] + term
        for place in range(21):
            r.short_parts[(chunk * 2 + side) * 24 + place] = sums[place]


def short_sums(r):
    total = jnp.sum(r.short_parts[...], axis=1)
    gather = ones_where(iota((LANES, LANES), 1) == iota((LANES, LANES), 0) // 16)
    high = total.astype(BF16)
    low = (total - high.astype(F32)).astype(BF16)
    grouped = dot(high, gather) + dot(low, gather)
    for side in range(2):
        total = None
        for block in range(16):
            first = (16 * side + block) * 24
            strip = grouped[first : first + 24]
            strip = pltpu.roll(strip, 8 * block, 1) if block else strip
            total = strip if total is None else total + strip
        for place in range(side, TEAM, 2):
            r.sum_mine[place, 8:11] = total[3 * (place // 2) : 3 * (place // 2) + 3]


def backward_chunk(r, chunk):
    for side, lanes in enumerate(halves()):
        totals = [[], [], []]
        for part in range(3):
            r.grads[chunk, part, side, COUNT:] = r.grad_halo[chunk, part, :, lanes].astype(F32)
        for strip in strips(32):
            masks = [r.back_short[lag, strip] for lag in range(6)]
            for part in range(3):
                window = lambda lag: r.grads[chunk, part, side, strip.start + lag : strip.stop + lag]
                totals[part].append(filter_strip(r, chunk, part, lanes, window, masks))
        rows = pl.ds(pl.multiple_of(chunk * WIDE + LANES * side, LANES), LANES)
        for part in range(3):
            r.out[part, rows] = jnp.transpose(jnp.concatenate(totals[part], axis=0)).astype(BF16)


OPERANDS = ["lengths", "raw_hbm", "short", "medium", "span", "cot_hbm"]
RESULTS = ["out", "short_out", "medium_out"]


def scratch(cap, chunks, groups):
    vmem = pltpu.VMEM
    dma = pltpu.SemaphoreType.DMA
    return {
        "raw": vmem((chunks, 3, cap, WIDE), BF16),
        "cot": vmem((chunks, WIDE, COUNT), BF16),
        "tail_out": vmem((chunks, TAIL_ROWS // 16, 16, WIDE), BF16),
        "edges": vmem((chunks, 8, 16, WIDE), BF16),
        "own_pick": vmem((LEAD + COUNT, cap), BF16),
        "edge_pick": vmem((3 * (FIRST_ROWS + LAST_ROWS), LANES), F32),
        "tail_pick": vmem((TAIL_ROWS, 3 * (cap - LATE)), BF16),
        "fore_short": vmem((6, COUNT, LANES), F32),
        "back_short": vmem((6, COUNT, LANES), F32),
        "taps": vmem((chunks, 3, 8, WIDE), F32),
        "rows": vmem((chunks, 3, 2, LEAD + COUNT, LANES), F32),
        "filtered": vmem((chunks, 2, COUNT, WIDE), F32),
        "cot_rows": vmem((chunks, COUNT, WIDE), F32),
        "mixed": vmem((chunks, HALF + COUNT, WIDE), BF16),
        "weighted": vmem((chunks, COUNT + HALF, WIDE), BF16),
        "fore_rows": vmem((groups, LANES), F32),
        "back_rows": vmem((groups, LANES), F32),
        "fore_mask": vmem((2, HALF, LANES), BF16),
        "back_mask": vmem((2, HALF, LANES), BF16),
        "back_mask32": vmem((2, HALF, LANES), F32),
        "grads": vmem((chunks, 3, 2, COUNT + 16, LANES), F32),
        "grad_head": vmem((chunks, 3, HEAD_ROWS, WIDE), BF16),
        "grad_halo": vmem((chunks, 3, HEAD_ROWS, WIDE), BF16),
        "corr": vmem((groups, 8, LANES), F32),
        "short_parts": vmem((chunks * 2 * 24, 8, LANES), F32),
        "live_out": vmem((2, 8, LANES), I32),
        "live_near": vmem((INNER, 8, LANES), I32),
        "live_far": vmem((INNER, 8, LANES), I32),
        "sum_mine": vmem((TEAM, 11, LANES), F32),
        "sum_first": vmem((TEAM, 11, LANES), F32),
        "sum_second": vmem((TEAM, 11, LANES), F32),
        "sum_all": vmem((TEAM, 11, LANES), F32),
        "short_all": vmem((24, groups), F32),
        "load_sem": dma((2, chunks)),
        "send_sem": dma((5,)),
        "recv_sem": dma((5, chunks)),
        "live_send": dma((2,)),
        "live_recv": dma((2,)),
        "sum_send": dma((3,)),
        "sum_recv": dma((3,)),
    }


def kernel(names, scale, *refs):
    r = types.SimpleNamespace(**dict(zip(names, refs)))
    r.cap = r.raw.shape[2]
    chunks = r.raw.shape[0]
    x, me = lax.axis_index("dp"), lax.axis_index("ctx")
    dp_count, ctx_count = lax.axis_size("dp"), lax.axis_size("ctx")
    right, left = lax.rem(me + 1, ctx_count), lax.rem(me + ctx_count - 1, ctx_count)
    row, col = lax.div(me, INNER), lax.rem(me, INNER)
    y, core = lax.div(col, 2), lax.rem(col, 2)
    place1, place2 = row * 2 + core, x * 4 + y

    def near_peer(hop):
        return {"ctx": row * INNER + lax.rem(col + hop, INNER)}

    def far_peer(hop):
        return {"ctx": lax.rem(row + hop, INNER) * INNER + col}

    def peer1(other):
        return {"dp": x, "ctx": lax.div(other, 2) * INNER + y * 2 + lax.rem(other, 2)}

    def peer2(other):
        return {"dp": lax.div(other, 4), "ctx": row * INNER + lax.rem(other, 4) * 2 + core}

    def remote(src, dst, send, recv, device):
        return pltpu.make_async_remote_copy(
            src, dst, send, recv, device_id=device, device_id_type=MESH
        )

    def load_raw(c):
        lanes = pl.ds(pl.multiple_of(c * WIDE, WIDE), WIDE)
        return pltpu.make_async_copy(r.raw_hbm.at[:, :, lanes], r.raw.at[c], r.load_sem.at[0, c])

    def load_cot(c):
        rows = pl.ds(pl.multiple_of(c * WIDE, WIDE), WIDE)
        return pltpu.make_async_copy(r.cot_hbm.at[rows], r.cot.at[c], r.load_sem.at[1, c])

    def send_tail(c):
        dst = r.edges.at[c, 0 : TAIL_ROWS // 16]
        return remote(r.tail_out.at[c], dst, r.send_sem.at[0], r.recv_sem.at[0, c], {"ctx": right})

    def send_head(c):
        src, dst = r.raw.at[c, :, 0:HEAD_ROWS], r.edges.at[c, TAIL_ROWS // 16 : 8]
        return remote(src, dst, r.send_sem.at[1], r.recv_sem.at[1, c], {"ctx": left})

    def send_mixed(c):
        src, dst = r.mixed.at[c, COUNT : COUNT + HALF], r.mixed.at[c, 0:HALF]
        return remote(src, dst, r.send_sem.at[2], r.recv_sem.at[2, c], {"ctx": right})

    def send_weighted(c):
        src, dst = r.weighted.at[c, 0:HALF], r.weighted.at[c, COUNT : COUNT + HALF]
        return remote(src, dst, r.send_sem.at[3], r.recv_sem.at[3, c], {"ctx": left})

    def send_grad(c):
        src, dst = r.grad_head.at[c], r.grad_halo.at[c]
        return remote(src, dst, r.send_sem.at[4], r.recv_sem.at[4, c], {"ctx": left})

    def live_copies(stage):
        near = stage == 0
        inbox = r.live_near if near else r.live_far
        return [
            remote(
                r.live_out.at[stage],
                inbox.at[INNER - hop],
                r.live_send.at[stage],
                r.live_recv.at[stage],
                near_peer(hop) if near else far_peer(hop),
            )
            for hop in range(1, INNER)
        ]

    def sum_copies(stage, source, target, peer, place):
        copies = []
        for hop in range(1, TEAM):
            other = lax.rem(place + hop, TEAM)
            copies.append(
                remote(
                    source(other),
                    target(TEAM - hop),
                    r.sum_send.at[stage],
                    r.sum_recv.at[stage],
                    peer(other),
                )
            )
        return copies

    def start(copies):
        for copy in copies:
            copy.start()

    def take(ref, sem):
        pltpu.make_async_copy(ref, ref, sem).wait()

    def finish_live(stage):
        some = r.live_near.at[1:INNER]
        take(some, r.live_send.at[stage])
        take(some, r.live_recv.at[stage])

    def finish_sum(stage):
        some = r.sum_first.at[1:TEAM]
        take(some, r.sum_send.at[stage])
        take(some, r.sum_recv.at[stage])

    def each(step, first=0, last=chunks):
        def body(c, carry):
            step(c)
            return carry

        lax.fori_loop(first, last, body, 0)

    barrier = pltpu.get_barrier_semaphore()
    peers = [{"ctx": right}, {"ctx": left}]
    peers += [near_peer(hop) for hop in range(1, INNER)]
    peers += [far_peer(hop) for hop in range(1, INNER)]
    peers += [{"dp": lax.rem(x + hop, dp_count)} for hop in range(1, dp_count)]

    def loads(c):
        load_raw(c).start()

    each(loads)
    for peer in peers:
        pl.semaphore_signal(barrier, inc=1, device_id=peer, device_id_type=MESH)

    def cot_loads(c):
        load_cot(c).start()

    each(cot_loads)
    live = r.lengths[0, 0] + r.lengths[0, 1]
    r.live_out[0] = jnp.zeros((8, LANES), I32) + live
    build_tail_pick(r)
    pl.semaphore_wait(barrier, len(peers))
    start(live_copies(0))

    def edges(c):
        for k in range(2):
            load_raw(2 * c + k).wait()
            send_head(2 * c + k).start()
        for k in range(2):
            tail_chunk(r, 2 * c + k)
        for k in range(2):
            send_tail(2 * c + k).start()

    each(edges, 0, chunks // 4)
    finish_live(0)
    ahead = jnp.zeros((8, LANES), I32)
    whole = r.live_out[0]
    for hop in range(1, INNER):
        value = r.live_near[hop]
        whole = whole + value
        ahead = ahead + value * jnp.where(col + hop >= INNER, 1, 0)
    r.live_out[1] = whole
    start(live_copies(1))

    each(edges, chunks // 4, chunks // 2)
    build_tables(r)

    def widen(c):
        for k in range(4):
            widen_taps(r, 4 * c + k)
        for k in range(4):
            load_cot(4 * c + k).wait()

    each(widen, 0, chunks // 4)
    finish_live(1)
    for hop in range(1, INNER):
        ahead = ahead + r.live_far[hop] * jnp.where(row + hop >= INNER, 1, 0)
    build_picks(r, ahead[0:1, 0:1] - me * COUNT)

    def forward(c):
        send_tail(c).wait_recv()
        send_head(c).wait_recv()
        forward_chunk(r, c)
        send_mixed(c).start()
        send_weighted(c).start()

    each(forward)

    def medium(c):
        send_mixed(c).wait_recv()
        send_weighted(c).wait_recv()
        medium_chunk(r, c)
        send_grad(c).start()
        short_sums_chunk(r, c)

    each(medium)
    medium_sums(r)
    short_sums(r)
    spread_out = sum_copies(
        0, lambda o: r.sum_mine.at[o], lambda h: r.sum_first.at[h], peer1, place1
    )
    start(spread_out)

    def backward(c):
        send_grad(c).wait_recv()
        backward_chunk(r, c)

    each(backward, 0, chunks * 3 // 8)
    finish_sum(0)
    total = r.sum_mine[place1]
    for hop in range(1, TEAM):
        total = total + r.sum_first[hop]
    r.sum_second[0] = total
    across = sum_copies(
        1, lambda o: r.sum_second.at[0], lambda h: r.sum_second.at[h], peer2, place2
    )
    start(across)
    each(backward, chunks * 3 // 8, chunks * 3 // 4)
    finish_sum(1)
    total = jnp.zeros((11, LANES), F32)
    for other in range(TEAM):
        total = total + r.sum_second[lax.rem(other - place2 + TEAM, TEAM)]
    r.sum_all[place1] = total * (1.0 / scale)
    handed = sum_copies(
        2, lambda o: r.sum_all.at[place1], lambda h: r.sum_all.at[place1], peer1, place1
    )
    start(handed)
    each(backward, chunks * 3 // 4, chunks)
    finish_sum(2)
    for place in range(TEAM):
        strip, side = place // 2, place % 2
        lanes = slice(LANES * side, LANES * side + LANES)
        r.medium_out[8 * strip : 8 * strip + 8, lanes] = r.sum_all[place, 0:8]
        r.short_all[3 * strip : 3 * strip + 3, lanes] = r.sum_all[place, 8:11]
    for part in range(3):
        r.short_out[part] = r.short_all[7 * part : 7 * part + 7]

    take(r.tail_out, r.send_sem.at[0])
    take(r.grad_head, r.send_sem.at[1])
    take(r.mixed.at[:, 0:HALF], r.send_sem.at[2])
    take(r.weighted.at[:, 0:HALF], r.send_sem.at[3])
    take(r.grad_head, r.send_sem.at[4])


def shards(raw_qkv, block_lengths, short_filter, medium_filter, doc_span, cotangent):
    count = cotangent.shape[2]
    width = cotangent.shape[1]
    groups = medium_filter.shape[0]
    group_size = width // groups
    raw = jnp.transpose(raw_qkv[0], (0, 2, 1))
    short = jnp.transpose(short_filter, (0, 2, 1))
    filt = jnp.transpose(medium_filter)
    scale = math.sqrt(lax.axis_size("dp") * lax.axis_size("ctx") * count * group_size)
    space = scratch(raw.shape[1], width // WIDE, groups)
    vmem = pl.BlockSpec(memory_space=pltpu.VMEM)
    anywhere = pl.BlockSpec(memory_space=pl.ANY)
    out, short_sum, medium_sum = pl.pallas_call(
        functools.partial(kernel, OPERANDS + RESULTS + list(space), scale),
        in_specs=[pl.BlockSpec(memory_space=pltpu.SMEM), anywhere, vmem, vmem, vmem, anywhere],
        out_specs=[vmem, vmem, vmem],
        out_shape=[
            pltpu.VMEM((3, width, count), BF16),
            jax.ShapeDtypeStruct((3, 7, groups), F32),
            jax.ShapeDtypeStruct((64, groups), F32),
        ],
        scratch_shapes=list(space.values()),
        compiler_params=pltpu.CompilerParams(
            collective_id=0, has_side_effects=True, vmem_limit_bytes=56 * 1024 * 1024
        ),
    )(block_lengths[0], raw, short, filt, doc_span[0], cotangent[0])
    return (out[None], jnp.transpose(short_sum, (0, 2, 1)), jnp.transpose(medium_sum))


def solution(mesh):
    return jax.shard_map(
        shards,
        mesh=mesh,
        in_specs=(
            P("dp", None, None, "ctx"),
            P("dp", "ctx", None),
            P(),
            P(),
            P("dp", None, "ctx"),
            P("dp", None, "ctx"),
        ),
        out_specs=(P("dp", None, None, "ctx"), P(), P()),
        check_vma=False,
    )
```

```python
import functools
import math
import types

import jax
import jax.numpy as jnp
from jax import lax
from jax.experimental import pallas as pl
from jax.experimental.pallas import tpu as pltpu
from jax.sharding import PartitionSpec as P

F32 = jnp.float32
BF16 = jnp.bfloat16
I32 = jnp.int32
MESH = pl.DeviceIdType.MESH
LANES = 128
WIDE = 256
LATE = 64
REACH = 22
TAIL_ROWS = 80
HEAD_ROWS = 16
LEAD = 8
HALF = 64
FIRST_ROWS = 24
LAST_ROWS = 16
COUNT = 128
TEAM = 16
INNER = 8


def iota(shape, dim):
    return lax.broadcasted_iota(I32, shape, dim)


def ones_where(condition, dtype=BF16):
    return jnp.where(condition, 1.0, 0.0).astype(dtype)


def dot(left, right):
    return jnp.dot(left, right, preferred_element_type=F32)


def dot_columns(left, right):
    return lax.dot_general(left, right, (((0,), (0,)), ((), ())), preferred_element_type=F32)


def column_of(row):
    return jnp.transpose(jnp.broadcast_to(row, (LANES, LANES)))


def halves():
    return [slice(LANES * side, LANES * side + LANES) for side in range(WIDE // LANES)]


def build_tail_pick(r):
    live = r.lengths[0, 0] + r.lengths[0, 1]
    rows = r.cap - LATE
    shape = (TAIL_ROWS, 3 * rows)
    place, column = iota(shape, 0), iota(shape, 1)
    pick = None
    for part in range(3):
        step = place - REACH * part
        own = (step >= 0) & (step < REACH) & (column - rows * part == live - REACH + step - LATE)
        pick = own if pick is None else pick | own
    r.tail_pick[...] = ones_where(pick)


def build_tables(r):
    before, after = column_of(r.span[0:1]), column_of(r.span[1:2])
    for lag in range(1, 7):
        r.fore_short[lag - 1] = ones_where(before >= lag, F32)
        r.back_short[lag - 1] = ones_where(after >= lag, F32)
    taps = r.medium.shape[0]
    source = iota((taps, LANES), 0)
    lane = iota((taps, LANES), 1)
    filt = r.medium[...].astype(BF16)
    r.fore_rows[...] = dot_columns(filt, ones_where(lane == taps - source))
    r.back_rows[...] = dot_columns(filt, ones_where(lane == source))
    row = iota((HALF, LANES), 0)
    lane = iota((HALF, LANES), 1)
    for half in range(2):
        part = slice(HALF * half, HALF * half + HALF)
        lag = row + HALF - lane
        r.fore_mask[half] = ones_where((lag >= 0) & (lag < taps) & (lag <= before[part]))
        lag = lane - row
        back = (lag >= 0) & (lag < taps) & (lag <= after[part])
        r.back_mask[half] = ones_where(back)
        r.back_mask32[half] = ones_where(back, F32)


def widen_taps(r, chunk):
    span = LANES * 16 // WIDE
    owner = lax.rem(chunk, span) * (WIDE // 16) + iota((LANES, WIDE), 1) // 16
    spread = ones_where(iota((LANES, WIDE), 0) == owner)
    window = pl.ds(pl.multiple_of(lax.div(chunk, span) * LANES, LANES), LANES)
    blank = jnp.zeros((1, LANES), F32)
    taps = [row for part in range(3) for row in (r.short[part, :, window], blank)]
    wide = dot(jnp.concatenate(taps, axis=0).astype(BF16), spread)
    for part in range(3):
        r.taps[chunk, part] = wide[8 * part : 8 * part + 8]


def tail_chunk(r, chunk):
    total = dot(r.tail_pick[...], r.raw[chunk, :, LATE:].reshape(3 * (r.cap - LATE), WIDE))
    r.tail_out[chunk] = total.astype(BF16).reshape(TAIL_ROWS // 16, 16, WIDE)


def build_picks(r, drift):
    live = r.lengths[0, 0] + r.lengths[0, 1]
    shape = (LEAD + COUNT, r.cap)
    token = iota(shape, 0) - LEAD - jnp.broadcast_to(drift, shape)
    column = iota(shape, 1)
    r.own_pick[...] = ones_where((column == token) & (column < live))
    shape = (FIRST_ROWS, LANES)
    token = iota(shape, 0) - LEAD - jnp.broadcast_to(drift, shape)
    column = iota(shape, 1)
    for part in range(3):
        late = token + REACH
        from_tail = (late >= 0) & (late < REACH) & (column == REACH * part + late)
        r.edge_pick[FIRST_ROWS * part : FIRST_ROWS * part + FIRST_ROWS] = ones_where(from_tail, F32)
    shape = (LAST_ROWS, LANES)
    token = iota(shape, 0) + COUNT - LAST_ROWS - jnp.broadcast_to(drift, shape)
    column = iota(shape, 1)
    for part in range(3):
        over = token - live
        from_head = (over >= 0) & (column == TAIL_ROWS + HEAD_ROWS * part + over)
        first = 3 * FIRST_ROWS + LAST_ROWS * part
        r.edge_pick[first : first + LAST_ROWS] = ones_where(from_head, F32)


def strips(rows):
    return [slice(first, first + rows) for first in range(0, COUNT, rows)]


def filter_strip(r, chunk, part, lanes, window, masks):
    total = r.taps[chunk, part, 0:1, lanes] * window(0)
    for lag in range(1, 7):
        total = total + r.taps[chunk, part, lag : lag + 1, lanes] * (masks[lag - 1] * window(lag))
    return total


def forward_chunk(r, chunk):
    edges = dot(r.edge_pick[...].astype(BF16), r.edges[chunk].reshape(COUNT, WIDE))
    for part in range(3):
        packed = dot(r.own_pick[...], r.raw[chunk, part])
        first = packed[:FIRST_ROWS] + edges[FIRST_ROWS * part : FIRST_ROWS * part + FIRST_ROWS]
        place = 3 * FIRST_ROWS + LAST_ROWS * part
        last = packed[LEAD + COUNT - LAST_ROWS :] + edges[place : place + LAST_ROWS]
        middle = packed[FIRST_ROWS : LEAD + COUNT - LAST_ROWS]
        for side, lanes in enumerate(halves()):
            r.rows[chunk, part, side, :FIRST_ROWS] = first[:, lanes]
            r.rows[chunk, part, side, FIRST_ROWS : LEAD + COUNT - LAST_ROWS] = middle[:, lanes]
            r.rows[chunk, part, side, LEAD + COUNT - LAST_ROWS :] = last[:, lanes]
    for side, lanes in enumerate(halves()):
        cot = jnp.transpose(r.cot[chunk, lanes]).astype(F32)
        r.cot_rows[chunk, :, lanes] = cot
        for strip in strips(32):
            masks = [r.fore_short[lag, strip] for lag in range(6)]
            query, key, value = [
                filter_strip(
                    r,
                    chunk,
                    part,
                    lanes,
                    lambda lag: r.rows[chunk, part, side, LEAD + strip.start - lag : LEAD + strip.stop - lag],
                    masks,
                )
                for part in range(3)
            ]
            r.filtered[chunk, 0, strip, lanes] = key
            r.filtered[chunk, 1, strip, lanes] = value
            r.mixed[chunk, HALF + strip.start : HALF + strip.stop, lanes] = (key * value).astype(BF16)
            r.weighted[chunk, strip, lanes] = (cot[strip] * query).astype(BF16)


def toeplitz(rows, g):
    row = jnp.broadcast_to(rows[g : g + 1], (HALF, LANES)).astype(BF16)
    return pltpu.roll(row, 0, 1, stride=1, stride_axis=0)


def own_lanes(every, pair_of):
    result = every[:HALF]
    for pair in range(1, 4):
        result = jnp.where(pair_of == pair, every[HALF * pair : HALF * pair + HALF], result)
    return result


def paired(bands, mask):
    bands = [band * mask for band in bands]
    pairs = [jnp.concatenate(bands[2 * p : 2 * p + 2], axis=1) for p in range(4)]
    return jnp.concatenate(pairs, axis=0)


def medium_chunk(r, chunk):
    shape = (HALF + COUNT, LANES)
    even = iota(shape, 1) // 16 % 2 == 0
    pair_of = iota((HALF, LANES), 1) // 32
    for side, lanes in enumerate(halves()):
        first = pl.multiple_of(chunk * 16 + 8 * side, 8)
        fore = r.fore_rows[pl.ds(first, 8)]
        back = r.back_rows[pl.ds(first, 8)]
        fores = [toeplitz(fore, g) for g in range(8)]
        backs = [toeplitz(back, g) for g in range(8)]
        mixed = r.mixed[chunk, :, lanes]
        weighted = r.weighted[chunk, :, lanes]
        zero = jnp.zeros(shape, BF16)
        mixed_of = [jnp.where(even, mixed, zero), jnp.where(even, zero, mixed)]
        weighted_of = [jnp.where(even, weighted, zero), jnp.where(even, zero, weighted)]
        corr = [None] * 8
        for half in range(2):
            part = slice(HALF * half, HALF * half + HALF)
            window = slice(HALF * half, HALF * half + 2 * HALF)
            earlier = jnp.concatenate([m[window] for m in mixed_of], axis=0)
            later = jnp.concatenate([w[window] for w in weighted_of], axis=0)
            response = own_lanes(dot(paired(fores, r.fore_mask[half]), earlier), pair_of)
            spread = own_lanes(dot(paired(backs, r.back_mask[half]), later), pair_of)
            grads = (
                r.cot_rows[chunk, part, lanes] * response,
                spread * r.filtered[chunk, 1, part, lanes],
                spread * r.filtered[chunk, 0, part, lanes],
            )
            if half == 0:
                heads = [grad[:8] for grad in grads] + [jnp.zeros((8, LANES), F32)]
                r.grad_head[chunk, :, lanes] = jnp.concatenate(heads, axis=0).astype(BF16)
            for b in range(3):
                grad = grads[b].astype(BF16)
                r.grads[chunk, b, side, part] = grad.astype(F32)
            own = mixed[HALF + HALF * half : 2 * HALF + HALF * half]
            alone = [jnp.where(pair_of == p, own, zero[:HALF]) for p in range(4)]
            turned = jnp.transpose(weighted[window])
            blank = jnp.zeros((16, LANES), BF16)
            sides = []
            for parity in range(2):
                blocks = [turned[16 * g : 16 * g + 16] if g % 2 == parity else blank for g in range(8)]
                sides.append(jnp.concatenate(blocks, axis=0))
            every = dot(jnp.concatenate(alone, axis=0), jnp.concatenate(sides, axis=1))
            mask = r.back_mask32[half]
            for g in range(8):
                tile = every[HALF * (g // 2) : HALF * (g // 2) + HALF]
                term = tile[:, LANES * (g % 2) : LANES * (g % 2) + LANES] * mask
                corr[g] = term if half == 0 else corr[g] + term
        for g in range(8):
            total = corr[g][0:8]
            for strip in range(1, 8):
                total = total + pltpu.roll(corr[g][8 * strip : 8 * strip + 8], LANES - 8 * strip, 1)
            r.corr[first + g] = total


def medium_sums(r):
    total = None
    for row in range(8):
        strip = r.corr[:, row, :]
        strip = strip if row == 0 else pltpu.roll(strip, LANES - row, 1)
        total = strip if total is None else total + strip
    total = jnp.transpose(total)
    for place in range(TEAM):
        strip, side = place // 2, place % 2
        r.sum_mine[place, 0:8] = total[8 * strip : 8 * strip + 8, LANES * side : LANES * side + LANES]


def short_sums_chunk(r, chunk):
    for side, lanes in enumerate(halves()):
        sums = [None] * 24
        for strip in strips(16):
            masks = [r.fore_short[lag, strip] for lag in range(6)]
            for part in range(3):
                grad = r.grads[chunk, part, side, strip]
                for lag in range(7):
                    window = r.rows[chunk, part, side, LEAD + strip.start - lag : LEAD + strip.stop - lag]
                    term = grad * window if lag == 0 else (masks[lag - 1] * grad) * window
                    term = term[0:8] + term[8:16]
                    place = 7 * part + lag
                    sums[place] = term if sums[place] is None else sums[place] + term
        for place in range(21):
            r.short_parts[(chunk * 2 + side) * 24 + place] = sums[place]


def short_sums(r):
    total = jnp.sum(r.short_parts[...], axis=1)
    gather = ones_where(iota((LANES, LANES), 1) == iota((LANES, LANES), 0) // 16)
    high = total.astype(BF16)
    low = (total - high.astype(F32)).astype(BF16)
    grouped = dot(high, gather) + dot(low, gather)
    for side in range(2):
        total = None
        for block in range(16):
            first = (16 * side + block) * 24
            strip = grouped[first : first + 24]
            strip = pltpu.roll(strip, 8 * block, 1) if block else strip
            total = strip if total is None else total + strip
        for place in range(side, TEAM, 2):
            r.sum_mine[place, 8:11] = total[3 * (place // 2) : 3 * (place // 2) + 3]


def backward_chunk(r, chunk):
    for side, lanes in enumerate(halves()):
        totals = [[], [], []]
        halo = r.grad_halo[chunk, :, lanes].astype(F32)
        for part in range(3):
            r.grads[chunk, part, side, COUNT : COUNT + 8] = halo[8 * part : 8 * part + 8]
        for strip in strips(32):
            masks = [r.back_short[lag, strip] for lag in range(6)]
            for part in range(3):
                window = lambda lag: r.grads[chunk, part, side, strip.start + lag : strip.stop + lag]
                totals[part].append(filter_strip(r, chunk, part, lanes, window, masks))
        rows = pl.ds(pl.multiple_of(chunk * WIDE + LANES * side, LANES), LANES)
        for part in range(3):
            r.out[part, rows] = jnp.transpose(jnp.concatenate(totals[part], axis=0).astype(BF16))


OPERANDS = ["lengths", "raw_hbm", "short", "medium", "span", "cot_hbm"]
RESULTS = ["out", "short_out", "medium_out"]


def scratch(cap, chunks, groups):
    vmem = pltpu.VMEM
    dma = pltpu.SemaphoreType.DMA
    return {
        "raw": vmem((chunks, 3, cap, WIDE), BF16),
        "cot": vmem((chunks, WIDE, COUNT), BF16),
        "tail_out": vmem((chunks, TAIL_ROWS // 16, 16, WIDE), BF16),
        "edges": vmem((chunks, 8, 16, WIDE), BF16),
        "own_pick": vmem((LEAD + COUNT, cap), BF16),
        "edge_pick": vmem((3 * (FIRST_ROWS + LAST_ROWS), LANES), F32),
        "tail_pick": vmem((TAIL_ROWS, 3 * (cap - LATE)), BF16),
        "fore_short": vmem((6, COUNT, LANES), F32),
        "back_short": vmem((6, COUNT, LANES), F32),
        "taps": vmem((chunks, 3, 8, WIDE), F32),
        "rows": vmem((chunks, 3, 2, LEAD + COUNT, LANES), F32),
        "filtered": vmem((chunks, 2, COUNT, WIDE), F32),
        "cot_rows": vmem((chunks, COUNT, WIDE), F32),
        "mixed": vmem((chunks, HALF + COUNT, WIDE), BF16),
        "weighted": vmem((chunks, COUNT + HALF, WIDE), BF16),
        "fore_rows": vmem((groups, LANES), F32),
        "back_rows": vmem((groups, LANES), F32),
        "fore_mask": vmem((2, HALF, LANES), BF16),
        "back_mask": vmem((2, HALF, LANES), BF16),
        "back_mask32": vmem((2, HALF, LANES), F32),
        "grads": vmem((chunks, 3, 2, COUNT + 16, LANES), F32),
        "grad_head": vmem((chunks, 32, WIDE), BF16),
        "grad_halo": vmem((chunks, 32, WIDE), BF16),
        "corr": vmem((groups, 8, LANES), F32),
        "short_parts": vmem((chunks * 2 * 24, 8, LANES), F32),
        "live_out": vmem((2, 8, LANES), I32),
        "live_near": vmem((INNER, 8, LANES), I32),
        "live_far": vmem((INNER, 8, LANES), I32),
        "sum_mine": vmem((TEAM, 11, LANES), F32),
        "sum_first": vmem((TEAM, 11, LANES), F32),
        "sum_second": vmem((TEAM, 11, LANES), F32),
        "sum_all": vmem((TEAM, 11, LANES), F32),
        "short_all": vmem((24, groups), F32),
        "load_sem": dma((2, chunks)),
        "send_sem": dma((5,)),
        "recv_sem": dma((5, chunks)),
        "live_send": dma((2,)),
        "live_recv": dma((2,)),
        "sum_send": dma((3,)),
        "sum_recv": dma((3,)),
    }


def kernel(names, scale, *refs):
    r = types.SimpleNamespace(**dict(zip(names, refs)))
    r.cap = r.raw.shape[2]
    chunks = r.raw.shape[0]
    x, me = lax.axis_index("dp"), lax.axis_index("ctx")
    dp_count, ctx_count = lax.axis_size("dp"), lax.axis_size("ctx")
    right, left = lax.rem(me + 1, ctx_count), lax.rem(me + ctx_count - 1, ctx_count)
    row, col = lax.div(me, INNER), lax.rem(me, INNER)
    y, core = lax.div(col, 2), lax.rem(col, 2)
    place1, place2 = row * 2 + core, x * 4 + y

    def near_peer(hop):
        return {"ctx": row * INNER + lax.rem(col + hop, INNER)}

    def far_peer(hop):
        return {"ctx": lax.rem(row + hop, INNER) * INNER + col}

    def peer1(other):
        return {"dp": x, "ctx": lax.div(other, 2) * INNER + y * 2 + lax.rem(other, 2)}

    def peer2(other):
        return {"dp": lax.div(other, 4), "ctx": row * INNER + lax.rem(other, 4) * 2 + core}

    def remote(src, dst, send, recv, device):
        return pltpu.make_async_remote_copy(
            src, dst, send, recv, device_id=device, device_id_type=MESH
        )

    def load_raw(c):
        lanes = pl.ds(pl.multiple_of(c * WIDE, WIDE), WIDE)
        return pltpu.make_async_copy(r.raw_hbm.at[:, :, lanes], r.raw.at[c], r.load_sem.at[0, c])

    def load_cot(c):
        rows = pl.ds(pl.multiple_of(c * WIDE, WIDE), WIDE)
        return pltpu.make_async_copy(r.cot_hbm.at[rows], r.cot.at[c], r.load_sem.at[1, c])

    def send_tail(c):
        dst = r.edges.at[c, 0 : TAIL_ROWS // 16]
        return remote(r.tail_out.at[c], dst, r.send_sem.at[0], r.recv_sem.at[0, c], {"ctx": right})

    def send_head(c):
        src, dst = r.raw.at[c, :, 0:HEAD_ROWS], r.edges.at[c, TAIL_ROWS // 16 : 8]
        return remote(src, dst, r.send_sem.at[1], r.recv_sem.at[1, c], {"ctx": left})

    def send_mixed(c):
        src, dst = r.mixed.at[c, COUNT : COUNT + HALF], r.mixed.at[c, 0:HALF]
        return remote(src, dst, r.send_sem.at[2], r.recv_sem.at[2, c], {"ctx": right})

    def send_weighted(c):
        src, dst = r.weighted.at[c, 0:HALF], r.weighted.at[c, COUNT : COUNT + HALF]
        return remote(src, dst, r.send_sem.at[3], r.recv_sem.at[3, c], {"ctx": left})

    def send_grad(c):
        src, dst = r.grad_head.at[c], r.grad_halo.at[c]
        return remote(src, dst, r.send_sem.at[4], r.recv_sem.at[4, c], {"ctx": left})

    def live_copies(stage):
        near = stage == 0
        inbox = r.live_near if near else r.live_far
        return [
            remote(
                r.live_out.at[stage],
                inbox.at[INNER - hop],
                r.live_send.at[stage],
                r.live_recv.at[stage],
                near_peer(hop) if near else far_peer(hop),
            )
            for hop in range(1, INNER)
        ]

    def sum_copies(stage, source, target, peer, place):
        copies = []
        for hop in range(1, TEAM):
            other = lax.rem(place + hop, TEAM)
            copies.append(
                remote(
                    source(other),
                    target(TEAM - hop),
                    r.sum_send.at[stage],
                    r.sum_recv.at[stage],
                    peer(other),
                )
            )
        return copies

    def start(copies):
        for copy in copies:
            copy.start()

    def take(ref, sem):
        pltpu.make_async_copy(ref, ref, sem).wait()

    def finish_live(stage):
        some = r.live_near.at[1:INNER]
        take(some, r.live_send.at[stage])
        take(some, r.live_recv.at[stage])

    def finish_sum(stage):
        some = r.sum_first.at[1:TEAM]
        take(some, r.sum_send.at[stage])
        take(some, r.sum_recv.at[stage])

    def each(step, first=0, last=chunks):
        def body(c, carry):
            step(c)
            return carry

        lax.fori_loop(first, last, body, 0)

    barrier = pltpu.get_barrier_semaphore()
    peers = [{"ctx": right}, {"ctx": left}]
    peers += [near_peer(hop) for hop in range(1, INNER)]
    peers += [far_peer(hop) for hop in range(1, INNER)]
    peers += [{"dp": lax.rem(x + hop, dp_count)} for hop in range(1, dp_count)]

    def loads(c):
        load_raw(c).start()

    each(loads)
    for peer in peers:
        pl.semaphore_signal(barrier, inc=1, device_id=peer, device_id_type=MESH)

    def cot_loads(c):
        load_cot(c).start()

    each(cot_loads)
    live = r.lengths[0, 0] + r.lengths[0, 1]
    r.live_out[0] = jnp.zeros((8, LANES), I32) + live
    build_tail_pick(r)
    pl.semaphore_wait(barrier, len(peers))
    start(live_copies(0))

    def edges(c):
        for k in range(2):
            load_raw(2 * c + k).wait()
            send_head(2 * c + k).start()
        for k in range(2):
            tail_chunk(r, 2 * c + k)
        for k in range(2):
            send_tail(2 * c + k).start()

    each(edges, 0, chunks // 4)
    finish_live(0)
    ahead = jnp.zeros((8, LANES), I32)
    whole = r.live_out[0]
    for hop in range(1, INNER):
        value = r.live_near[hop]
        whole = whole + value
        ahead = ahead + value * jnp.where(col + hop >= INNER, 1, 0)
    r.live_out[1] = whole
    start(live_copies(1))

    each(edges, chunks // 4, chunks // 2)
    build_tables(r)

    def widen(c):
        for k in range(4):
            widen_taps(r, 4 * c + k)
        for k in range(4):
            load_cot(4 * c + k).wait()

    each(widen, 0, chunks // 4)
    finish_live(1)
    for hop in range(1, INNER):
        ahead = ahead + r.live_far[hop] * jnp.where(row + hop >= INNER, 1, 0)
    build_picks(r, ahead[0:1, 0:1] - me * COUNT)

    def forward(c):
        send_tail(c).wait_recv()
        send_head(c).wait_recv()
        forward_chunk(r, c)
        send_mixed(c).start()
        send_weighted(c).start()

    each(forward)

    def medium(c):
        send_mixed(c).wait_recv()
        send_weighted(c).wait_recv()
        medium_chunk(r, c)
        send_grad(c).start()
        short_sums_chunk(r, c)

    each(medium)
    medium_sums(r)
    short_sums(r)
    spread_out = sum_copies(
        0, lambda o: r.sum_mine.at[o], lambda h: r.sum_first.at[h], peer1, place1
    )
    start(spread_out)

    def backward(c):
        send_grad(c).wait_recv()
        backward_chunk(r, c)

    each(backward, 0, chunks * 3 // 8)
    finish_sum(0)
    total = r.sum_mine[place1]
    for hop in range(1, TEAM):
        total = total + r.sum_first[hop]
    r.sum_second[0] = total
    across = sum_copies(
        1, lambda o: r.sum_second.at[0], lambda h: r.sum_second.at[h], peer2, place2
    )
    start(across)
    each(backward, chunks * 3 // 8, chunks * 3 // 4)
    finish_sum(1)
    total = jnp.zeros((11, LANES), F32)
    for other in range(TEAM):
        total = total + r.sum_second[lax.rem(other - place2 + TEAM, TEAM)]
    r.sum_all[place1] = total * (1.0 / scale)
    handed = sum_copies(
        2, lambda o: r.sum_all.at[place1], lambda h: r.sum_all.at[place1], peer1, place1
    )
    start(handed)
    each(backward, chunks * 3 // 4, chunks)
    finish_sum(2)
    for place in range(TEAM):
        strip, side = place // 2, place % 2
        lanes = slice(LANES * side, LANES * side + LANES)
        r.medium_out[8 * strip : 8 * strip + 8, lanes] = r.sum_all[place, 0:8]
        r.short_all[3 * strip : 3 * strip + 3, lanes] = r.sum_all[place, 8:11]
    for part in range(3):
        r.short_out[part] = r.short_all[7 * part : 7 * part + 7]

    take(r.tail_out, r.send_sem.at[0])
    take(r.edges.at[:, TAIL_ROWS // 16 : 8], r.send_sem.at[1])
    take(r.mixed.at[:, 0:HALF], r.send_sem.at[2])
    take(r.weighted.at[:, 0:HALF], r.send_sem.at[3])
    take(r.grad_head, r.send_sem.at[4])


def shards(raw_qkv, block_lengths, short_filter, medium_filter, doc_span, cotangent):
    count = cotangent.shape[2]
    width = cotangent.shape[1]
    groups = medium_filter.shape[0]
    group_size = width // groups
    raw = jnp.transpose(raw_qkv[0], (0, 2, 1))
    short = jnp.transpose(short_filter, (0, 2, 1))
    filt = jnp.transpose(medium_filter)
    scale = math.sqrt(lax.axis_size("dp") * lax.axis_size("ctx") * count * group_size)
    space = scratch(raw.shape[1], width // WIDE, groups)
    vmem = pl.BlockSpec(memory_space=pltpu.VMEM)
    anywhere = pl.BlockSpec(memory_space=pl.ANY)
    out, short_sum, medium_sum = pl.pallas_call(
        functools.partial(kernel, OPERANDS + RESULTS + list(space), scale),
        in_specs=[pl.BlockSpec(memory_space=pltpu.SMEM), anywhere, vmem, vmem, vmem, anywhere],
        out_specs=[vmem, vmem, vmem],
        out_shape=[
            pltpu.VMEM((3, width, count), BF16),
            jax.ShapeDtypeStruct((3, 7, groups), F32),
            jax.ShapeDtypeStruct((64, groups), F32),
        ],
        scratch_shapes=list(space.values()),
        compiler_params=pltpu.CompilerParams(
            collective_id=0, has_side_effects=True, vmem_limit_bytes=56 * 1024 * 1024
        ),
    )(block_lengths[0], raw, short, filt, doc_span[0], cotangent[0])
    return (out[None], jnp.transpose(short_sum, (0, 2, 1)), jnp.transpose(medium_sum))


def solution(mesh):
    return jax.shard_map(
        shards,
        mesh=mesh,
        in_specs=(
            P("dp", None, None, "ctx"),
            P("dp", "ctx", None),
            P(),
            P(),
            P("dp", None, "ctx"),
            P("dp", None, "ctx"),
        ),
        out_specs=(P("dp", None, None, "ctx"), P(), P()),
        check_vma=False,
    )
```

```python
import functools
import math
import types

import jax
import jax.numpy as jnp
from jax import lax
from jax.experimental import pallas as pl
from jax.experimental.pallas import tpu as pltpu
from jax.sharding import PartitionSpec as P

F32 = jnp.float32
BF16 = jnp.bfloat16
I32 = jnp.int32
MESH = pl.DeviceIdType.MESH
LANES = 128
WIDE = 256
LATE = 64
REACH = 22
TAIL_ROWS = 80
HEAD_ROWS = 16
LEAD = 8
HALF = 64
FIRST_ROWS = 24
LAST_ROWS = 16
COUNT = 128
TEAM = 16
INNER = 8


def iota(shape, dim):
    return lax.broadcasted_iota(I32, shape, dim)


def ones_where(condition, dtype=BF16):
    return jnp.where(condition, 1.0, 0.0).astype(dtype)


def dot(left, right):
    return jnp.dot(left, right, preferred_element_type=F32)


def dot_columns(left, right):
    return lax.dot_general(left, right, (((0,), (0,)), ((), ())), preferred_element_type=F32)


def column_of(row):
    return jnp.transpose(jnp.broadcast_to(row, (LANES, LANES)))


def halves():
    return [slice(LANES * side, LANES * side + LANES) for side in range(WIDE // LANES)]


def build_tail_pick(r):
    live = r.lengths[0, 0] + r.lengths[0, 1]
    rows = r.cap - LATE
    shape = (TAIL_ROWS, 3 * rows)
    place, column = iota(shape, 0), iota(shape, 1)
    pick = None
    for part in range(3):
        step = place - REACH * part
        own = (step >= 0) & (step < REACH) & (column - rows * part == live - REACH + step - LATE)
        pick = own if pick is None else pick | own
    r.tail_pick[...] = ones_where(pick)


def build_tables(r):
    before, after = column_of(r.span[0:1]), column_of(r.span[1:2])
    for lag in range(1, 7):
        r.fore_short[lag - 1] = ones_where(before >= lag, F32)
        r.back_short[lag - 1] = ones_where(after >= lag, F32)
    taps = r.medium.shape[0]
    source = iota((taps, LANES), 0)
    lane = iota((taps, LANES), 1)
    filt = r.medium[...].astype(BF16)
    r.fore_rows[...] = dot_columns(filt, ones_where(lane == taps - source))
    r.back_rows[...] = dot_columns(filt, ones_where(lane == source))
    row = iota((HALF, LANES), 0)
    lane = iota((HALF, LANES), 1)
    for half in range(2):
        part = slice(HALF * half, HALF * half + HALF)
        lag = row + HALF - lane
        r.fore_mask[half] = ones_where((lag >= 0) & (lag < taps) & (lag <= before[part]))
        lag = lane - row
        back = (lag >= 0) & (lag < taps) & (lag <= after[part])
        r.back_mask[half] = ones_where(back)
        r.back_mask32[half] = ones_where(back, F32)


def widen_taps(r, chunk):
    span = LANES * 16 // WIDE
    owner = lax.rem(chunk, span) * (WIDE // 16) + iota((LANES, WIDE), 1) // 16
    spread = ones_where(iota((LANES, WIDE), 0) == owner)
    window = pl.ds(pl.multiple_of(lax.div(chunk, span) * LANES, LANES), LANES)
    blank = jnp.zeros((1, LANES), F32)
    taps = [row for part in range(3) for row in (r.short[part, :, window], blank)]
    wide = dot(jnp.concatenate(taps, axis=0).astype(BF16), spread)
    for part in range(3):
        r.taps[chunk, part] = wide[8 * part : 8 * part + 8]


def tail_chunk(r, chunk):
    total = dot(r.tail_pick[...], r.raw[chunk, :, LATE:].reshape(3 * (r.cap - LATE), WIDE))
    r.tail_out[chunk] = total.astype(BF16).reshape(TAIL_ROWS // 16, 16, WIDE)


def build_picks(r, drift):
    live = r.lengths[0, 0] + r.lengths[0, 1]
    shape = (LEAD + COUNT, r.cap)
    token = iota(shape, 0) - LEAD - jnp.broadcast_to(drift, shape)
    column = iota(shape, 1)
    r.own_pick[...] = ones_where((column == token) & (column < live))
    shape = (FIRST_ROWS, LANES)
    token = iota(shape, 0) - LEAD - jnp.broadcast_to(drift, shape)
    column = iota(shape, 1)
    for part in range(3):
        late = token + REACH
        from_tail = (late >= 0) & (late < REACH) & (column == REACH * part + late)
        r.edge_pick[FIRST_ROWS * part : FIRST_ROWS * part + FIRST_ROWS] = ones_where(from_tail, F32)
    shape = (LAST_ROWS, LANES)
    token = iota(shape, 0) + COUNT - LAST_ROWS - jnp.broadcast_to(drift, shape)
    column = iota(shape, 1)
    for part in range(3):
        over = token - live
        from_head = (over >= 0) & (column == TAIL_ROWS + HEAD_ROWS * part + over)
        first = 3 * FIRST_ROWS + LAST_ROWS * part
        r.edge_pick[first : first + LAST_ROWS] = ones_where(from_head, F32)


def strips(rows):
    return [slice(first, first + rows) for first in range(0, COUNT, rows)]


def filter_strip(r, chunk, part, lanes, window, masks):
    total = r.taps[chunk, part, 0:1, lanes] * window(0)
    for lag in range(1, 7):
        total = total + r.taps[chunk, part, lag : lag + 1, lanes] * (masks[lag - 1] * window(lag))
    return total


def forward_chunk(r, chunk):
    edges = dot(r.edge_pick[...].astype(BF16), r.edges[chunk].reshape(COUNT, WIDE))
    for part in range(3):
        packed = dot(r.own_pick[...], r.raw[chunk, part])
        first = packed[:FIRST_ROWS] + edges[FIRST_ROWS * part : FIRST_ROWS * part + FIRST_ROWS]
        place = 3 * FIRST_ROWS + LAST_ROWS * part
        last = packed[LEAD + COUNT - LAST_ROWS :] + edges[place : place + LAST_ROWS]
        middle = packed[FIRST_ROWS : LEAD + COUNT - LAST_ROWS]
        for side, lanes in enumerate(halves()):
            r.rows[chunk, part, side, :FIRST_ROWS] = first[:, lanes]
            r.rows[chunk, part, side, FIRST_ROWS : LEAD + COUNT - LAST_ROWS] = middle[:, lanes]
            r.rows[chunk, part, side, LEAD + COUNT - LAST_ROWS :] = last[:, lanes]
    for side, lanes in enumerate(halves()):
        cot = jnp.transpose(r.cot[chunk, lanes]).astype(F32)
        r.cot_rows[chunk, :, lanes] = cot
        for strip in strips(32):
            masks = [r.fore_short[lag, strip] for lag in range(6)]
            query, key, value = [
                filter_strip(
                    r,
                    chunk,
                    part,
                    lanes,
                    lambda lag: r.rows[chunk, part, side, LEAD + strip.start - lag : LEAD + strip.stop - lag],
                    masks,
                )
                for part in range(3)
            ]
            r.filtered[chunk, 0, strip, lanes] = key
            r.filtered[chunk, 1, strip, lanes] = value
            r.mixed[chunk, HALF + strip.start : HALF + strip.stop, lanes] = (key * value).astype(BF16)
            r.weighted[chunk, strip, lanes] = (cot[strip] * query).astype(BF16)


def toeplitz(rows, g):
    row = jnp.broadcast_to(rows[g : g + 1], (HALF, LANES)).astype(BF16)
    return pltpu.roll(row, 0, 1, stride=1, stride_axis=0)


def own_lanes(every, pair_of):
    result = every[:HALF]
    for pair in range(1, 4):
        result = jnp.where(pair_of == pair, every[HALF * pair : HALF * pair + HALF], result)
    return result


def paired(bands, mask):
    bands = [band * mask for band in bands]
    pairs = [jnp.concatenate(bands[2 * p : 2 * p + 2], axis=1) for p in range(4)]
    return jnp.concatenate(pairs, axis=0)


def medium_chunk(r, chunk):
    shape = (HALF + COUNT, LANES)
    even = iota(shape, 1) // 16 % 2 == 0
    pair_of = iota((HALF, LANES), 1) // 32
    for side, lanes in enumerate(halves()):
        first = pl.multiple_of(chunk * 16 + 8 * side, 8)
        fore = r.fore_rows[pl.ds(first, 8)]
        back = r.back_rows[pl.ds(first, 8)]
        fores = [toeplitz(fore, g) for g in range(8)]
        backs = [toeplitz(back, g) for g in range(8)]
        mixed = r.mixed[chunk, :, lanes]
        weighted = r.weighted[chunk, :, lanes]
        zero = jnp.zeros(shape, BF16)
        mixed_of = [jnp.where(even, mixed, zero), jnp.where(even, zero, mixed)]
        weighted_of = [jnp.where(even, weighted, zero), jnp.where(even, zero, weighted)]
        corr = [None] * 8
        for half in range(2):
            part = slice(HALF * half, HALF * half + HALF)
            window = slice(HALF * half, HALF * half + 2 * HALF)
            earlier = jnp.concatenate([m[window] for m in mixed_of], axis=0)
            later = jnp.concatenate([w[window] for w in weighted_of], axis=0)
            response = own_lanes(dot(paired(fores, r.fore_mask[half]), earlier), pair_of)
            spread = own_lanes(dot(paired(backs, r.back_mask[half]), later), pair_of)
            grads = (
                r.cot_rows[chunk, part, lanes] * response,
                spread * r.filtered[chunk, 1, part, lanes],
                spread * r.filtered[chunk, 0, part, lanes],
            )
            if half == 0:
                heads = [grad[:8] for grad in grads] + [jnp.zeros((8, LANES), F32)]
                r.grad_head[chunk, :, lanes] = jnp.concatenate(heads, axis=0).astype(BF16)
            for b in range(3):
                grad = grads[b].astype(BF16)
                r.grads[chunk, b, side, part] = grad.astype(F32)
            own = mixed[HALF + HALF * half : 2 * HALF + HALF * half]
            alone = [jnp.where(pair_of == p, own, zero[:HALF]) for p in range(4)]
            turned = jnp.transpose(weighted[window])
            blank = jnp.zeros((16, LANES), BF16)
            sides = []
            for parity in range(2):
                blocks = [turned[16 * g : 16 * g + 16] if g % 2 == parity else blank for g in range(8)]
                sides.append(jnp.concatenate(blocks, axis=0))
            every = dot(jnp.concatenate(alone, axis=0), jnp.concatenate(sides, axis=1))
            mask = r.back_mask32[half]
            for g in range(8):
                tile = every[HALF * (g // 2) : HALF * (g // 2) + HALF]
                term = tile[:, LANES * (g % 2) : LANES * (g % 2) + LANES] * mask
                corr[g] = term if half == 0 else corr[g] + term
        for g in range(8):
            total = corr[g][0:8]
            for strip in range(1, 8):
                total = total + pltpu.roll(corr[g][8 * strip : 8 * strip + 8], LANES - 8 * strip, 1)
            r.corr[first + g] = total


def medium_sums(r):
    total = None
    for row in range(8):
        strip = r.corr[:, row, :]
        strip = strip if row == 0 else pltpu.roll(strip, LANES - row, 1)
        total = strip if total is None else total + strip
    total = jnp.transpose(total)
    for place in range(TEAM):
        strip, side = place // 2, place % 2
        r.sum_mine[place, 0:8] = total[8 * strip : 8 * strip + 8, LANES * side : LANES * side + LANES]


def short_sums_chunk(r, chunk):
    for side, lanes in enumerate(halves()):
        sums = [None] * 24
        for strip in strips(16):
            masks = [r.fore_short[lag, strip] for lag in range(6)]
            for part in range(3):
                grad = r.grads[chunk, part, side, strip]
                for lag in range(7):
                    window = r.rows[chunk, part, side, LEAD + strip.start - lag : LEAD + strip.stop - lag]
                    term = grad * window if lag == 0 else (masks[lag - 1] * grad) * window
                    term = term[0:8] + term[8:16]
                    place = 7 * part + lag
                    sums[place] = term if sums[place] is None else sums[place] + term
        for place in range(21):
            r.short_parts[(chunk * 2 + side) * 24 + place] = sums[place]


def short_sums(r):
    total = jnp.sum(r.short_parts[...], axis=1)
    gather = ones_where(iota((LANES, LANES), 1) == iota((LANES, LANES), 0) // 16)
    high = total.astype(BF16)
    low = (total - high.astype(F32)).astype(BF16)
    grouped = dot(high, gather) + dot(low, gather)
    for side in range(2):
        total = None
        for block in range(16):
            first = (16 * side + block) * 24
            strip = grouped[first : first + 24]
            strip = pltpu.roll(strip, 8 * block, 1) if block else strip
            total = strip if total is None else total + strip
        for place in range(side, TEAM, 2):
            r.sum_mine[place, 8:11] = total[3 * (place // 2) : 3 * (place // 2) + 3]


def backward_chunk(r, chunk):
    for side, lanes in enumerate(halves()):
        totals = [[], [], []]
        halo = r.grad_halo[chunk, :, lanes].astype(F32)
        for part in range(3):
            r.grads[chunk, part, side, COUNT : COUNT + 8] = halo[8 * part : 8 * part + 8]
        for strip in strips(32):
            masks = [r.back_short[lag, strip] for lag in range(6)]
            for part in range(3):
                window = lambda lag: r.grads[chunk, part, side, strip.start + lag : strip.stop + lag]
                totals[part].append(filter_strip(r, chunk, part, lanes, window, masks))
        rows = pl.ds(pl.multiple_of(chunk * WIDE + LANES * side, LANES), LANES)
        for part in range(3):
            r.out[part, rows] = jnp.transpose(jnp.concatenate(totals[part], axis=0).astype(BF16))


OPERANDS = ["lengths", "raw_hbm", "short", "medium", "span", "cot_hbm"]
RESULTS = ["out", "short_out", "medium_out"]


def scratch(cap, chunks, groups):
    vmem = pltpu.VMEM
    dma = pltpu.SemaphoreType.DMA
    return {
        "raw": vmem((chunks, 3, cap, WIDE), BF16),
        "cot": vmem((chunks, WIDE, COUNT), BF16),
        "tail_out": vmem((chunks, TAIL_ROWS // 16, 16, WIDE), BF16),
        "edges": vmem((chunks, 8, 16, WIDE), BF16),
        "own_pick": vmem((LEAD + COUNT, cap), BF16),
        "edge_pick": vmem((3 * (FIRST_ROWS + LAST_ROWS), LANES), F32),
        "tail_pick": vmem((TAIL_ROWS, 3 * (cap - LATE)), BF16),
        "fore_short": vmem((6, COUNT, LANES), F32),
        "back_short": vmem((6, COUNT, LANES), F32),
        "taps": vmem((chunks, 3, 8, WIDE), F32),
        "rows": vmem((chunks, 3, 2, LEAD + COUNT, LANES), F32),
        "filtered": vmem((chunks, 2, COUNT, WIDE), F32),
        "cot_rows": vmem((chunks, COUNT, WIDE), F32),
        "mixed": vmem((chunks, HALF + COUNT, WIDE), BF16),
        "weighted": vmem((chunks, COUNT + HALF, WIDE), BF16),
        "fore_rows": vmem((groups, LANES), F32),
        "back_rows": vmem((groups, LANES), F32),
        "fore_mask": vmem((2, HALF, LANES), BF16),
        "back_mask": vmem((2, HALF, LANES), BF16),
        "back_mask32": vmem((2, HALF, LANES), F32),
        "grads": vmem((chunks, 3, 2, COUNT + 16, LANES), F32),
        "grad_head": vmem((chunks, 32, WIDE), BF16),
        "grad_halo": vmem((chunks, 32, WIDE), BF16),
        "corr": vmem((groups, 8, LANES), F32),
        "short_parts": vmem((chunks * 2 * 24, 8, LANES), F32),
        "live_out": vmem((2, 8, LANES), I32),
        "live_near": vmem((INNER, 8, LANES), I32),
        "live_far": vmem((INNER, 8, LANES), I32),
        "sum_mine": vmem((TEAM, 11, LANES), F32),
        "sum_first": vmem((TEAM, 11, LANES), F32),
        "sum_second": vmem((TEAM, 11, LANES), F32),
        "sum_all": vmem((TEAM, 11, LANES), F32),
        "short_all": vmem((24, groups), F32),
        "load_sem": dma((2, chunks)),
        "send_sem": dma((5,)),
        "recv_sem": dma((5, chunks)),
        "live_send": dma((2,)),
        "live_recv": dma((2,)),
        "sum_send": dma((3,)),
        "sum_recv": dma((3,)),
    }


def kernel(names, scale, *refs):
    r = types.SimpleNamespace(**dict(zip(names, refs)))
    r.cap = r.raw.shape[2]
    chunks = r.raw.shape[0]
    x, me = lax.axis_index("dp"), lax.axis_index("ctx")
    dp_count, ctx_count = lax.axis_size("dp"), lax.axis_size("ctx")
    right, left = lax.rem(me + 1, ctx_count), lax.rem(me + ctx_count - 1, ctx_count)
    row, col = lax.div(me, INNER), lax.rem(me, INNER)
    y, core = lax.div(col, 2), lax.rem(col, 2)
    place1, place2 = row * 2 + core, x * 4 + y

    def near_peer(hop):
        return {"ctx": row * INNER + lax.rem(col + hop, INNER)}

    def far_peer(hop):
        return {"ctx": lax.rem(row + hop, INNER) * INNER + col}

    def peer1(other):
        return {"dp": x, "ctx": lax.div(other, 2) * INNER + y * 2 + lax.rem(other, 2)}

    def peer2(other):
        return {"dp": lax.div(other, 4), "ctx": row * INNER + lax.rem(other, 4) * 2 + core}

    def remote(src, dst, send, recv, device):
        return pltpu.make_async_remote_copy(
            src, dst, send, recv, device_id=device, device_id_type=MESH
        )

    def load_raw(c):
        lanes = pl.ds(pl.multiple_of(c * WIDE, WIDE), WIDE)
        return pltpu.make_async_copy(r.raw_hbm.at[:, :, lanes], r.raw.at[c], r.load_sem.at[0, c])

    def load_cot(c):
        rows = pl.ds(pl.multiple_of(c * WIDE, WIDE), WIDE)
        return pltpu.make_async_copy(r.cot_hbm.at[rows], r.cot.at[c], r.load_sem.at[1, c])

    def send_tail(c):
        dst = r.edges.at[c, 0 : TAIL_ROWS // 16]
        return remote(r.tail_out.at[c], dst, r.send_sem.at[0], r.recv_sem.at[0, c], {"ctx": right})

    def send_head(c):
        src, dst = r.raw.at[c, :, 0:HEAD_ROWS], r.edges.at[c, TAIL_ROWS // 16 : 8]
        return remote(src, dst, r.send_sem.at[1], r.recv_sem.at[1, c], {"ctx": left})

    def send_mixed(c):
        src, dst = r.mixed.at[c, COUNT : COUNT + HALF], r.mixed.at[c, 0:HALF]
        return remote(src, dst, r.send_sem.at[2], r.recv_sem.at[2, c], {"ctx": right})

    def send_weighted(c):
        src, dst = r.weighted.at[c, 0:HALF], r.weighted.at[c, COUNT : COUNT + HALF]
        return remote(src, dst, r.send_sem.at[3], r.recv_sem.at[3, c], {"ctx": left})

    def send_grad(c):
        src, dst = r.grad_head.at[c], r.grad_halo.at[c]
        return remote(src, dst, r.send_sem.at[4], r.recv_sem.at[4, c], {"ctx": left})

    def live_copies(stage):
        near = stage == 0
        inbox = r.live_near if near else r.live_far
        return [
            remote(
                r.live_out.at[stage],
                inbox.at[INNER - hop],
                r.live_send.at[stage],
                r.live_recv.at[stage],
                near_peer(hop) if near else far_peer(hop),
            )
            for hop in range(1, INNER)
        ]

    def sum_copies(stage, source, target, peer, place):
        copies = []
        for hop in range(1, TEAM):
            other = lax.rem(place + hop, TEAM)
            copies.append(
                remote(
                    source(other),
                    target(TEAM - hop),
                    r.sum_send.at[stage],
                    r.sum_recv.at[stage],
                    peer(other),
                )
            )
        return copies

    def start(copies):
        for copy in copies:
            copy.start()

    def take(ref, sem):
        pltpu.make_async_copy(ref, ref, sem).wait()

    def finish_live(stage):
        some = r.live_near.at[1:INNER]
        take(some, r.live_send.at[stage])
        take(some, r.live_recv.at[stage])

    def finish_sum(stage):
        take(r.sum_first.at[1:TEAM], r.sum_recv.at[stage])

    def each(step, first=0, last=chunks):
        def body(c, carry):
            step(c)
            return carry

        lax.fori_loop(first, last, body, 0)

    barrier = pltpu.get_barrier_semaphore()
    peers = [{"ctx": right}, {"ctx": left}]
    peers += [near_peer(hop) for hop in range(1, INNER)]
    peers += [far_peer(hop) for hop in range(1, INNER)]
    peers += [{"dp": lax.rem(x + hop, dp_count)} for hop in range(1, dp_count)]

    def loads(c):
        load_raw(c).start()

    each(loads)
    for peer in peers:
        pl.semaphore_signal(barrier, inc=1, device_id=peer, device_id_type=MESH)

    def cot_loads(c):
        load_cot(c).start()

    each(cot_loads)
    live = r.lengths[0, 0] + r.lengths[0, 1]
    r.live_out[0] = jnp.zeros((8, LANES), I32) + live
    build_tail_pick(r)
    pl.semaphore_wait(barrier, len(peers))
    start(live_copies(0))

    def edges(c):
        for k in range(2):
            load_raw(2 * c + k).wait()
            send_head(2 * c + k).start()
        for k in range(2):
            tail_chunk(r, 2 * c + k)
        for k in range(2):
            send_tail(2 * c + k).start()

    each(edges, 0, chunks // 4)
    finish_live(0)
    ahead = jnp.zeros((8, LANES), I32)
    whole = r.live_out[0]
    for hop in range(1, INNER):
        value = r.live_near[hop]
        whole = whole + value
        ahead = ahead + value * jnp.where(col + hop >= INNER, 1, 0)
    r.live_out[1] = whole
    start(live_copies(1))

    each(edges, chunks // 4, chunks // 2)
    build_tables(r)

    def widen(c):
        for k in range(4):
            widen_taps(r, 4 * c + k)
        for k in range(4):
            load_cot(4 * c + k).wait()

    each(widen, 0, chunks // 4)
    finish_live(1)
    for hop in range(1, INNER):
        ahead = ahead + r.live_far[hop] * jnp.where(row + hop >= INNER, 1, 0)
    build_picks(r, ahead[0:1, 0:1] - me * COUNT)

    def forward(c):
        send_tail(c).wait_recv()
        send_head(c).wait_recv()
        forward_chunk(r, c)
        send_mixed(c).start()
        send_weighted(c).start()

    each(forward)

    def medium(c):
        send_mixed(c).wait_recv()
        send_weighted(c).wait_recv()
        medium_chunk(r, c)
        send_grad(c).start()
        short_sums_chunk(r, c)

    each(medium)
    medium_sums(r)
    short_sums(r)
    spread_out = sum_copies(
        0, lambda o: r.sum_mine.at[o], lambda h: r.sum_first.at[h], peer1, place1
    )
    start(spread_out)

    def backward(c):
        send_grad(c).wait_recv()
        backward_chunk(r, c)

    each(backward, 0, chunks * 5 // 16)
    finish_sum(0)
    total = r.sum_mine[place1]
    for hop in range(1, TEAM):
        total = total + r.sum_first[hop]
    r.sum_second[0] = total
    across = sum_copies(
        1, lambda o: r.sum_second.at[0], lambda h: r.sum_second.at[h], peer2, place2
    )
    start(across)
    each(backward, chunks * 5 // 16, chunks * 5 // 8)
    finish_sum(1)
    total = jnp.zeros((11, LANES), F32)
    for other in range(TEAM):
        total = total + r.sum_second[lax.rem(other - place2 + TEAM, TEAM)]
    r.sum_all[place1] = total * (1.0 / scale)
    handed = sum_copies(
        2, lambda o: r.sum_all.at[place1], lambda h: r.sum_all.at[place1], peer1, place1
    )
    start(handed)
    each(backward, chunks * 5 // 8, chunks)
    finish_sum(2)
    for place in range(TEAM):
        strip, side = place // 2, place % 2
        lanes = slice(LANES * side, LANES * side + LANES)
        r.medium_out[8 * strip : 8 * strip + 8, lanes] = r.sum_all[place, 0:8]
        r.short_all[3 * strip : 3 * strip + 3, lanes] = r.sum_all[place, 8:11]
    for part in range(3):
        r.short_out[part] = r.short_all[7 * part : 7 * part + 7]

    for stage in range(3):
        take(r.sum_first.at[1:TEAM], r.sum_send.at[stage])
    take(r.tail_out, r.send_sem.at[0])
    take(r.edges.at[:, TAIL_ROWS // 16 : 8], r.send_sem.at[1])
    take(r.mixed.at[:, 0:HALF], r.send_sem.at[2])
    take(r.weighted.at[:, 0:HALF], r.send_sem.at[3])
    take(r.grad_head, r.send_sem.at[4])


def shards(raw_qkv, block_lengths, short_filter, medium_filter, doc_span, cotangent):
    count = cotangent.shape[2]
    width = cotangent.shape[1]
    groups = medium_filter.shape[0]
    group_size = width // groups
    raw = jnp.transpose(raw_qkv[0], (0, 2, 1))
    short = jnp.transpose(short_filter, (0, 2, 1))
    filt = jnp.transpose(medium_filter)
    scale = math.sqrt(lax.axis_size("dp") * lax.axis_size("ctx") * count * group_size)
    space = scratch(raw.shape[1], width // WIDE, groups)
    vmem = pl.BlockSpec(memory_space=pltpu.VMEM)
    anywhere = pl.BlockSpec(memory_space=pl.ANY)
    out, short_sum, medium_sum = pl.pallas_call(
        functools.partial(kernel, OPERANDS + RESULTS + list(space), scale),
        in_specs=[pl.BlockSpec(memory_space=pltpu.SMEM), anywhere, vmem, vmem, vmem, anywhere],
        out_specs=[vmem, vmem, vmem],
        out_shape=[
            pltpu.VMEM((3, width, count), BF16),
            jax.ShapeDtypeStruct((3, 7, groups), F32),
            jax.ShapeDtypeStruct((64, groups), F32),
        ],
        scratch_shapes=list(space.values()),
        compiler_params=pltpu.CompilerParams(
            collective_id=0, has_side_effects=True, vmem_limit_bytes=56 * 1024 * 1024
        ),
    )(block_lengths[0], raw, short, filt, doc_span[0], cotangent[0])
    return (out[None], jnp.transpose(short_sum, (0, 2, 1)), jnp.transpose(medium_sum))


def solution(mesh):
    return jax.shard_map(
        shards,
        mesh=mesh,
        in_specs=(
            P("dp", None, None, "ctx"),
            P("dp", "ctx", None),
            P(),
            P(),
            P("dp", None, "ctx"),
            P("dp", None, "ctx"),
        ),
        out_specs=(P("dp", None, None, "ctx"), P(), P()),
        check_vma=False,
    )
```
